32 devices in a mesh: seq: 8 (over z, x), head: 4 (over y, core).
Axes of the slice: x: 2, y: 2, z: 4, core: 2. Of those that a mesh axis runs over, the one named last changes fastest.
Arguments:
- query_heads: bfloat16 [4, 4, 64, 192], P(None, None, 'head'), may hold values from -6 to 6
- up_keys: bfloat16 [64, 128, 512], P('head'), may hold values from -0.5 to 0.5
- up_values: bfloat16 [64, 512, 128], P('head'), may hold values from -0.25 to 0.25
- latent_cache: bfloat16 [4, 65536, 576], P(None, ('seq', 'head')), may hold values from -120 to 120
- new_latent: bfloat16 [4, 4, 576], replicated, may hold values from -24 to 24
- context_lengths: int32 [4], replicated, may hold values from 8192 to 65536, as said below
- positions: int32 [4], replicated, may hold values from 0 to 65535
Outputs:
- attended: bfloat16 [4, 4, 64, 128], P(None, None, 'head')
The draws below stay inside these ranges and needn't reach their ends.
Inputs may be any that keep to these rules, and one draw needn't show every extreme that they name: `context_lengths`: some request uses all 65536 cached positions.
All inputs are finite; a program needn't handle non-finite values.
Results may differ from the reference program's by a relative error of at most 0.019.
The reference program's roundings to bfloat16 on the way count: a program that leaves them out, or rounds other values in their place, can miss the bound.
Values may be sent and summed in bfloat16 or wider, within the bound.
A program may use at most 512 MiB of HBM per device.

```python
import jax
import jax.numpy as jnp
from jax import lax

HEADS = 64
NOPE = 128
ROPE = 64
KV = 512
VD = 128
BATCH = 4
STEPS = 4
CTX = 65536


def draw_latent_cache(key, part):
    key = jax.random.fold_in(key, 11)
    noise_key = jax.random.fold_in(key, 0)
    values = 2.0 * jnp.clip(jax.random.normal(noise_key, (BATCH, CTX, KV + ROPE), jnp.float32), -6.0, 6.0)
    return values.astype(jnp.bfloat16)


def draw_context_lengths(key, part):
    key = jax.random.fold_in(key, 23)
    length_key, longest_key = jax.random.split(key)
    lengths = jax.random.randint(length_key, (BATCH,), CTX // 8, CTX + 1, jnp.int32)
    longest = jax.random.randint(longest_key, (), 0, BATCH, jnp.int32)
    return jnp.where(jnp.arange(BATCH, dtype=jnp.int32) == longest, CTX, lengths).astype(jnp.int32)


def touch_ends(array, stream_key, smallest, largest):
    longest = array.shape.index(max(array.shape))
    spots = []
    for shift in (0, 1):
        where = [jax.random.randint(jax.random.fold_in(stream_key, axis), (), 0, length) for axis, length in enumerate(array.shape)]
        where[longest] = (where[longest] + shift) % array.shape[longest]
        spots.append(tuple(where))
    return array.at[spots[0]].set(smallest).at[spots[1]].set(largest)


def block_scale(key, extent, shards, low, top_value):
    def one(axis_at, shards_of):
        draws = jax.random.uniform(jax.random.fold_in(jax.random.fold_in(key, 6), axis_at), (shards_of,), jnp.float32, low / len(shards), top_value / len(shards))
        return jnp.repeat(jnp.exp(draws), extent[axis_at] // shards_of).reshape((-1,) + (1,) * (len(extent) - axis_at - 1))

    factor_of = one(*shards[0])
    for cut in shards[1:]:
        factor_of = factor_of * one(*cut)
    return factor_of


def noise(key, shape, scale, bound, pieces=(), kind=jnp.bfloat16):
    drawn = scale * jax.random.normal(key, shape, jnp.float32)
    if pieces:
        drawn = drawn * block_scale(key, shape, pieces, -0.22, 0.18)
    return jnp.clip(drawn, -bound, bound).astype(kind)


def setup_inputs(seed: int = 0) -> dict:
    keys = jax.random.split(jax.random.key(seed), 8)
    query_heads = noise(keys[0], (STEPS, BATCH, HEADS, NOPE + ROPE), 1.0, 6.0, ((2, 4),))
    up_keys = noise(keys[1], (HEADS, NOPE, KV), NOPE ** -0.5, 0.5, ((0, 4),))
    up_values = noise(keys[2], (HEADS, KV, VD), KV ** -0.5, 0.25, ((0, 4),))
    latent_cache = draw_latent_cache(jax.random.fold_in(keys[7], 71), 0)
    new_latent = noise(keys[4], (STEPS, BATCH, KV + ROPE), 4.0, 24.0)
    context_lengths = draw_context_lengths(jax.random.fold_in(keys[7], 71), 0)
    positions = touch_ends(jax.random.randint(keys[6], (BATCH,), 0, CTX), jax.random.fold_in(keys[6], 1), 0, CTX - 1).astype(jnp.int32)
    return {"query_heads": query_heads, "up_keys": up_keys, "up_values": up_values, "latent_cache": latent_cache, "new_latent": new_latent, "context_lengths": context_lengths, "positions": positions}


rope_base = 50000.0
masked_score = -1.0e30


def rotate(values, where_at):
    halfway = values.shape[-1] // 2
    counter = jnp.arange(halfway, dtype=jnp.float32)
    inverse = jnp.power(jnp.float32(rope_base), -2.0 * counter / values.shape[-1])
    angles = where_at.astype(jnp.float32)[..., None] * inverse
    cosine = jnp.cos(angles)
    sine_part = jnp.sin(angles)
    leading = values[..., :halfway]
    trailing = values[..., halfway:]
    return jnp.concatenate([leading * cosine - trailing * sine_part, trailing * cosine + leading * sine_part], axis=-1)


def build_new_keys(new_latent, pos_grid, latent_width):
    rotated = rotate(new_latent[..., latent_width:].astype(jnp.float32), pos_grid).astype(jnp.bfloat16)
    return jnp.concatenate([new_latent[..., :latent_width], rotated], axis=-1)


def reference(query_heads, up_keys, up_values, latent_cache, new_latent, context_lengths, positions):
    pos_grid = positions[None, :] + jnp.arange(STEPS, dtype=jnp.int32)[:, None]
    query_latent = jnp.einsum("sbhn,hnc->sbhc", query_heads[..., :NOPE].astype(jnp.float32), up_keys.astype(jnp.float32)).astype(jnp.bfloat16)
    query_rope = rotate(query_heads[..., NOPE:].astype(jnp.float32), pos_grid[:, :, None]).astype(jnp.bfloat16)
    queries = jnp.concatenate([query_latent, query_rope], axis=-1)
    new_keys = build_new_keys(new_latent, pos_grid, KV)
    softmax_scale = float(NOPE + ROPE) ** -0.5
    row_step = jnp.repeat(jnp.arange(STEPS, dtype=jnp.int32), HEADS)

    def one_request(request_item):
        query_block, cache_block, fresh_keys, length = request_item
        query_rows = query_block.reshape(STEPS * HEADS, KV + ROPE)
        all_keys = jnp.concatenate([cache_block, fresh_keys], axis=0)
        scores = jnp.dot(query_rows, all_keys.T, preferred_element_type=jnp.float32) * softmax_scale
        cache_visible = jnp.arange(CTX, dtype=jnp.int32) < length
        fresh_visible = jnp.arange(STEPS, dtype=jnp.int32)[None, :] <= row_step[:, None]
        visible = jnp.concatenate([jnp.broadcast_to(cache_visible[None, :], (STEPS * HEADS, CTX)), fresh_visible], axis=1)
        scores = jnp.where(visible, scores, masked_score)
        highest = jnp.max(scores, axis=1, keepdims=True)
        weights = jnp.where(visible, jnp.exp(scores - highest), 0.0)
        weight_sum = jnp.sum(weights, axis=1, keepdims=True)
        weighted = jnp.dot(weights.astype(jnp.bfloat16), all_keys[:, :KV], preferred_element_type=jnp.float32)
        return (weighted / weight_sum).reshape(STEPS, HEADS, KV)

    latent_out = lax.map(one_request, (jnp.swapaxes(queries, 0, 1), latent_cache, jnp.swapaxes(new_keys, 0, 1), context_lengths))
    return jnp.einsum("bshc,hcv->sbhv", latent_out.astype(jnp.float32), up_values.astype(jnp.float32), precision=lax.Precision.HIGHEST).astype(jnp.bfloat16)
```

```python
import functools

import jax
import jax.numpy as jnp
from jax import lax
from jax.experimental import pallas as pl
from jax.experimental.pallas import tpu as pltpu
from jax.sharding import PartitionSpec as P

MESH = pl.DeviceIdType.MESH
rope_base = 50000.0
masked_score = -1e30
lowest_peak = -1e29
log2_e = 1.4426950408889634
owners = 8
tile = 128
chunk = 512


def iota(shape, axis):
    return lax.broadcasted_iota(jnp.int32, shape, axis)


def rope_table(positions, steps, rope_width):
    halfway = rope_width // 2
    counter = jnp.arange(halfway, dtype=jnp.float32)
    inverse = jnp.power(jnp.float32(rope_base), -2.0 * counter / rope_width)
    grid = positions[None, :] + jnp.arange(steps, dtype=jnp.int32)[:, None]
    angles = grid.reshape(-1).astype(jnp.float32)[:, None] * inverse
    cosine, sine = jnp.cos(angles), jnp.sin(angles)
    return jnp.concatenate([cosine, cosine, -sine, sine], axis=-1)


def pack(values, peak, total):
    def term(v):
        return v.astype(jnp.bfloat16).astype(jnp.float32)

    p0 = term(peak)
    p1 = term(peak - p0)
    p2 = peak - p0 - p1
    t0 = term(total)
    t1 = total - t0
    shape = peak.shape[:-1] + (tile,)
    lane = iota(shape, len(shape) - 1)
    stats = jnp.where(lane == 0, p0, jnp.where(lane == 1, p1, jnp.where(lane == 2, p2, jnp.where(lane == 3, t0, t1))))
    return values.astype(jnp.bfloat16), stats.astype(jnp.bfloat16)


def unpack(packed, width):
    values = packed[..., :width].astype(jnp.float32)
    stats = packed[..., width:].astype(jnp.float32)
    peak = stats[..., 0:1] + stats[..., 1:2] + stats[..., 2:3]
    total = stats[..., 3:4] + stats[..., 4:5]
    return values, peak, total


def merge(one, two):
    (va, pa, ta), (vb, pb, tb) = one, two
    peak = jnp.maximum(pa, pb)
    wa, wb = jnp.exp2(pa - peak), jnp.exp2(pb - peak)
    return va * wa + vb * wb, peak, ta * wa + tb * wb


def kernel(
    seq_size,
    lengths,
    q_ref,
    new_ref,
    table_ref,
    up_keys_hbm,
    up_values_hbm,
    cache_hbm,
    out_ref,
    up_keys,
    up_values,
    cache,
    queries,
    new_keys,
    scores,
    partial,
    a_in,
    b_out,
    kept,
    b_in,
    c_out,
    c_in,
    gathered,
    load_sem,
    key_sem,
    value_sem,
    q1_send,
    q1_recv,
    qy_send,
    qy_recv,
    qf_send,
    qf_recv,
    a_send,
    a_recv,
    b_send,
    b_recv,
    c_send,
    c_recv,
    g_send,
    g_recv,
):
    steps, requests, heads, query_width = q_ref.shape
    nope, width = up_keys.shape[1], up_keys.shape[2]
    rope = query_width - nope
    rows_cached = cache.shape[1]
    rows = steps * heads
    piece = rows // owners
    all_rows = 4 * rows
    seq = lax.axis_index("seq")
    head = lax.axis_index("head")
    low = lax.rem(head, 2)
    high = lax.div(head, 2)
    near = head + 1 - 2 * low
    across = lax.rem(head + 2, 4)
    slot = seq * 4 + head
    owned = lax.rem(seq, owners)

    def at_head(h):
        return (seq, h)

    barrier = pltpu.get_barrier_semaphore()
    for h in (near, across):
        pl.semaphore_signal(barrier, inc=1, device_id=at_head(h), device_id_type=MESH)
    for d in range(1, seq_size):
        pl.semaphore_signal(barrier, inc=1, device_id=(lax.rem(seq + d, seq_size), head), device_id_type=MESH)

    key_load = pltpu.make_async_copy(up_keys_hbm, up_keys, key_sem)
    key_load.start()
    value_load = pltpu.make_async_copy(up_values_hbm.at[pl.ds(owned * 2, 2)], up_values, value_sem)

    def load(b):
        return pltpu.make_async_copy(cache_hbm.at[b], cache.at[b], load_sem.at[b])

    for b in range(requests):
        load(b).start()
    value_load.start()

    swap = (iota((rope, rope), 0) == lax.rem(iota((rope, rope), 1) + rope // 2, rope)).astype(jnp.bfloat16)
    cosine = table_ref[:, :rope]
    sine = table_ref[:, rope:]
    flat = q_ref[...].reshape(steps * requests * heads, query_width)
    q_rope = flat[:, nope:]
    swapped = jnp.dot(q_rope, swap, preferred_element_type=jnp.float32)
    three = (steps * requests, heads, rope)
    rotated = (
        q_rope.astype(jnp.float32).reshape(three) * cosine[:, None, :] + swapped.reshape(three) * sine[:, None, :]
    )
    rotated = rotated.astype(jnp.bfloat16).reshape(steps * requests * heads, rope)
    count = steps * requests * heads
    row = iota((count, count), 0)
    wanted = (row & (steps - 1)) * (requests * heads) + lax.div(row, rows) * heads + lax.div(lax.rem(row, rows), steps)
    order = (iota((count, count), 1) == wanted).astype(jnp.bfloat16)
    q_nope = jnp.dot(order, flat[:, :nope], preferred_element_type=jnp.float32).astype(jnp.bfloat16)
    rotated = jnp.dot(order, rotated, preferred_element_type=jnp.float32).astype(jnp.bfloat16)

    new_flat = new_ref[...]
    new_rope = new_flat[:, width:]
    new_swapped = jnp.dot(new_rope, swap, preferred_element_type=jnp.float32)
    new_rotated = new_rope.astype(jnp.float32) * cosine + new_swapped * sine
    new_keys[...] = jnp.zeros_like(new_keys)
    new_keys[: steps * requests, :width] = new_flat[:, :width]
    new_keys[: steps * requests, width:] = new_rotated.astype(jnp.bfloat16)

    own_head = lax.div(lax.rem(iota((count, nope), 0), rows), steps)
    spread = jnp.concatenate(
        [jnp.where(own_head == h, q_nope.astype(jnp.float32), 0.0).astype(jnp.bfloat16) for h in range(heads)], axis=1
    )
    key_load.wait()
    latent = jnp.dot(spread, up_keys[...].reshape(heads * nope, width), preferred_element_type=jnp.float32)
    latent = latent.astype(jnp.bfloat16)
    for b in range(requests):
        queries[b, head, :, :width] = latent[b * rows : (b + 1) * rows]
        queries[b, head, :, width:] = rotated[b * rows : (b + 1) * rows]

    def remote(source, target, send, recv, device):
        return pltpu.make_async_remote_copy(
            src_ref=source, dst_ref=target, send_sem=send, recv_sem=recv, device_id=device, device_id_type=MESH
        )

    def q_near(b):
        block = queries.at[b, head]
        return remote(block, block, q1_send.at[b], q1_recv.at[b], at_head(near))

    def q_across(b):
        block = queries.at[b, head]
        return remote(block, block, qy_send.at[b], qy_recv.at[b], at_head(across))

    def q_forward(b):
        block = queries.at[b, across]
        return remote(block, block, qf_send.at[b], qf_recv.at[b], at_head(near))

    def a_copy(b, j):
        return remote(
            partial.at[b, 1 - low + 2 * j], a_in.at[b, j], a_send.at[b, j], a_recv.at[b, j], at_head(near)
        )

    def b_copy(b):
        return remote(b_out.at[b], b_in.at[b], b_send.at[b], b_recv.at[b], at_head(across))

    def c_copy(p, target, source):
        return remote(
            c_out.at[p, target], c_in.at[p, source], c_send.at[p, target], c_recv.at[p, source], (target, head)
        )

    def g_copy(d):
        target = lax.rem(seq + d, seq_size)
        return remote(
            gathered.at[owned], gathered.at[owned], g_send.at[target], g_recv.at[owned], (target, head)
        )

    pl.semaphore_wait(barrier, 2 + seq_size - 1)
    for b in range(requests):
        q_across(b).start()
        q_near(b).start()

    q_across(0).wait_recv()
    q_forward(0).start()

    factor = log2_e * float(query_width) ** (-0.5)

    def attend(b):
        q_near(b).wait_recv()
        q_forward(b).wait_recv()
        load(b).wait()
        q = queries[b].reshape(all_rows, width + rope)
        length = lengths[b]
        peaks = jnp.full((all_rows, tile), lowest_peak, jnp.float32)

        def tiles(x, op, start):
            for i in range(x.shape[1] // tile):
                start = op(start, x[:, i * tile : (i + 1) * tile])
            return start

        nt = (((1,), (1,)), ((), ()))
        for c in range(rows_cached // chunk):
            s = lax.dot_general(
                q, cache[b, c * chunk : (c + 1) * chunk, :], nt, preferred_element_type=jnp.float32
            )
            number = slot * rows_cached + c * chunk + iota((1, chunk), 1)
            x = s * factor + jnp.where(number < length, 0.0, masked_score)
            scores[:, c * chunk : (c + 1) * chunk] = x
            peaks = tiles(x, jnp.maximum, peaks)
        s = lax.dot_general(q, new_keys[...], nt, preferred_element_type=jnp.float32)
        column = iota((all_rows, tile), 1)
        step = iota((all_rows, tile), 0) & (steps - 1)
        fresh = (
            (lax.rem(column, requests) == b)
            & (lax.div(column, requests) <= step)
            & (column < steps * requests)
            & (slot == 0)
        )
        x_new = s * factor + jnp.where(fresh, 0.0, masked_score)
        peak = jnp.max(jnp.maximum(peaks, x_new), axis=1, keepdims=True)

        @pl.when(b < requests - 1)
        def _():
            q_across(b + 1).wait_recv()
            q_forward(b + 1).start()

        weights = jnp.exp2(x_new - peak)
        totals = weights
        total_out = jnp.dot(weights.astype(jnp.bfloat16), new_keys[:, :width], preferred_element_type=jnp.float32)
        for c in range(rows_cached // chunk):
            weights = jnp.exp2(scores[:, c * chunk : (c + 1) * chunk] - peak)
            totals = tiles(weights, jnp.add, totals)
            total_out += jnp.dot(
                weights.astype(jnp.bfloat16),
                cache[b, c * chunk : (c + 1) * chunk, :width],
                preferred_element_type=jnp.float32,
            )
        total = jnp.sum(totals, axis=1, keepdims=True)
        values, stats = pack(total_out, peak, total)
        partial[b, :, :, :width] = values.reshape(4, rows, width)
        partial[b, :, :, width:] = stats.reshape(4, rows, tile)
        for j in range(2):
            a_copy(b, j).start()

    def merge_near(b):
        for j in range(2):
            a_copy(b, j).wait_recv()
        other = 1 - high
        merged = merge(
            unpack(partial[b, low + 2 * other], width),
            unpack(a_in[b, other], width),
        )
        values, stats = pack(*merged)
        b_out[b, :, :width] = values
        b_out[b, :, width:] = stats
        b_copy(b).start()
        values, peak, total = merge(
            unpack(partial[b, head], width),
            unpack(a_in[b, high], width),
        )
        kept[b, :, :width] = values
        kept[b, :, width:] = jnp.where(iota((rows, tile), 1) == 0, peak, total)

    def merge_across(b):
        b_copy(b).wait_recv()
        mine = (kept[b, :, :width], kept[b, :, width : width + 1], kept[b, :, width + 1 : width + 2])
        values, peak, total = merge(mine, unpack(b_in[b], width))
        kept[b, :, :width] = values
        kept[b, :, width:] = jnp.where(iota((rows, tile), 1) == 0, peak, total)

    def send_pair(p):
        both = jnp.concatenate(
            [kept[2 * p + i].reshape(owners, piece, width + tile) for i in range(2)], axis=1
        )
        values, stats = pack(both[..., :width], both[..., width : width + 1], both[..., width + 1 : width + 2])
        c_out[p, :, :, :width] = values
        c_out[p, :, :, width:] = stats
        for d in range(0 if seq_size > owners else 1, owners):
            target = lax.rem(seq + d, owners)
            if d == 0:
                @pl.when(seq >= owners)
                def _():
                    c_copy(p, target, seq).start()
            else:
                c_copy(p, target, seq).start()

    def finish_pair(p):
        c_in[p, owned] = c_out[p, owned]
        for d in range(1, seq_size):
            c_copy(p, owned, lax.rem(seq + d, seq_size)).wait_recv()
        values, peaks, totals = unpack(c_in[p], width)
        peak = jnp.max(peaks, axis=0, keepdims=True)
        scale = jnp.exp2(peaks - peak)
        mixed = jnp.sum(values * scale, axis=0) / jnp.sum(totals * scale, axis=0)
        both = 2 * piece
        second = lax.rem(iota((both, width), 0), piece) >= steps
        wide = jnp.concatenate([jnp.where(second, 0.0, mixed), jnp.where(second, mixed, 0.0)], axis=1)
        w0 = wide.astype(jnp.bfloat16)
        rest = wide - w0.astype(jnp.float32)
        w1 = rest.astype(jnp.bfloat16)
        w2 = (rest - w1.astype(jnp.float32)).astype(jnp.bfloat16)
        matrix = up_values[...].reshape(2 * width, up_values.shape[2])
        result = sum(jnp.dot(w, matrix, preferred_element_type=jnp.float32) for w in (w2, w1, w0))
        gathered[owned, p * both : (p + 1) * both, :] = result.astype(jnp.bfloat16)

    def body(b, carry):
        attend(b)

        @pl.when(b >= 1)
        def _():
            merge_near(b - 1)

        @pl.when(b >= 2)
        def _():
            merge_across(b - 2)

        @pl.when(b == requests - 1)
        def _():
            send_pair(0)

        return carry

    lax.fori_loop(0, requests, body, 0)
    merge_near(requests - 1)
    merge_across(requests - 2)
    value_load.wait()

    def when_owner(fn):
        if seq_size > owners:
            pl.when(seq < owners)(fn)
        else:
            fn()

    when_owner(lambda: finish_pair(0))
    merge_across(requests - 1)
    send_pair(1)

    def last():
        finish_pair(1)
        for d in range(1, seq_size):
            g_copy(d).start()

    when_owner(last)

    def from_owner(j):
        block = gathered.at[j]
        return remote(block, block, g_send.at[j], g_recv.at[j], (seq, near))

    for d in range(0 if seq_size > owners else 1, owners):
        source = lax.rem(seq + d, owners)
        if d == 0:
            @pl.when(seq >= owners)
            def _():
                from_owner(source).wait_recv()
        else:
            from_owner(source).wait_recv()

    per = rows * requests // owners
    row = iota((count, count), 0)
    s_of = lax.div(row, requests * heads)
    b_of = lax.rem(lax.div(row, heads), requests)
    h_of = lax.rem(row, heads)
    source = (
        lax.div(h_of, 2) * per + lax.div(b_of, 2) * (2 * piece) + (b_of & 1) * piece + (h_of & 1) * steps + s_of
    )
    back = (iota((count, count), 1) == source).astype(jnp.bfloat16)
    result = jnp.dot(back, gathered[...].reshape(count, -1), preferred_element_type=jnp.float32)
    out_ref[...] = result.astype(jnp.bfloat16).reshape(out_ref.shape)

    for b in range(requests):
        q_near(b).wait_send()
        q_across(b).wait_send()
        q_forward(b).wait_send()
        for j in range(2):
            a_copy(b, j).wait_send()
        b_copy(b).wait_send()
    for p in range(2):
        for d in range(0 if seq_size > owners else 1, owners):
            target = lax.rem(seq + d, owners)
            if d == 0:
                @pl.when(seq >= owners)
                def _():
                    c_copy(p, target, seq).wait_send()
            else:
                c_copy(p, target, seq).wait_send()

    def sent():
        for d in range(1, seq_size):
            g_copy(d).wait_send()

    when_owner(sent)


def on_device(seq_size, query_heads, up_keys, up_values, latent_cache, new_latent, context_lengths, positions):
    steps, requests, heads, query_width = query_heads.shape
    nope, width = up_keys.shape[1:]
    value_width = up_values.shape[2]
    key_width = latent_cache.shape[2]
    cached = latent_cache.shape[1]
    rows = steps * heads
    table = rope_table(positions, steps, query_width - nope)
    bf16, f32 = jnp.bfloat16, jnp.float32
    packed = width + tile
    dma = pltpu.SemaphoreType.DMA
    vmem = pl.BlockSpec(memory_space=pltpu.VMEM)
    anywhere = pl.BlockSpec(memory_space=pl.ANY)
    return pl.pallas_call(
        functools.partial(kernel, seq_size),
        out_shape=jax.ShapeDtypeStruct((steps, requests, heads, value_width), bf16),
        in_specs=[pl.BlockSpec(memory_space=pltpu.SMEM), vmem, vmem, vmem, anywhere, anywhere, anywhere],
        out_specs=vmem,
        scratch_shapes=[
            pltpu.VMEM((heads, nope, width), bf16),
            pltpu.VMEM((2, width, value_width), bf16),
            pltpu.VMEM((requests, cached, key_width), bf16),
            pltpu.VMEM((requests, 4, rows, key_width), bf16),
            pltpu.VMEM((tile, key_width), bf16),
            pltpu.VMEM((4 * rows, cached), f32),
            pltpu.VMEM((requests, 4, rows, packed), bf16),
            pltpu.VMEM((requests, 2, rows, packed), bf16),
            pltpu.VMEM((requests, rows, packed), bf16),
            pltpu.VMEM((requests, rows, packed), f32),
            pltpu.VMEM((requests, rows, packed), bf16),
            pltpu.VMEM((2, owners, 2 * rows // owners, packed), bf16),
            pltpu.VMEM((2, seq_size, 2 * rows // owners, packed), bf16),
            pltpu.VMEM((owners, requests * rows // owners, value_width), bf16),
            dma((requests,)),
            dma,
            dma,
        ]
        + [dma((requests,))] * 6
        + [dma((requests, 2))] * 2
        + [dma((requests,))] * 2
        + [dma((2, owners)), dma((2, seq_size)), dma((seq_size,)), dma((owners,))],
        compiler_params=pltpu.CompilerParams(
            collective_id=0, has_side_effects=True, vmem_limit_bytes=56 * 1024 * 1024
        ),
        cost_estimate=pl.CostEstimate(
            flops=2 * requests * 4 * rows * cached * (key_width + width),
            bytes_accessed=2 * requests * cached * key_width,
            transcendentals=requests * 4 * rows * cached,
        ),
    )(
        context_lengths,
        query_heads,
        new_latent.reshape(steps * requests, key_width),
        table,
        up_keys,
        up_values,
        latent_cache,
    )


def solution(mesh):
    in_specs = (
        P(None, None, "head", None),
        P("head", None, None),
        P("head", None, None),
        P(None, ("seq", "head"), None),
        P(),
        P(),
        P(),
    )
    out_specs = P(None, None, "head", None)
    return jax.shard_map(
        functools.partial(on_device, mesh.shape["seq"]),
        mesh=mesh,
        in_specs=in_specs,
        out_specs=out_specs,
        check_vma=False,
    )
```

```python
import functools

import jax
import jax.numpy as jnp
import numpy as np
from jax import lax
from jax.experimental import pallas as pl
from jax.experimental.pallas import tpu as pltpu
from jax.sharding import PartitionSpec as P

MESH = pl.DeviceIdType.MESH
rope_base = 50000.0
masked_score = -1e30
lowest_peak = -1e29
log2_e = 1.4426950408889634
owners = 8
tile = 128
chunk = 512
turn_high = np.float32(6.28125)
turn_middle = np.float32(254 / 128 / 1024)
turn_low = np.float32(2 * np.pi - 6.28125 - 254 / 128 / 1024)


def iota(shape, axis):
    return lax.broadcasted_iota(jnp.int32, shape, axis)


def frequencies(rope_width):
    halfway = rope_width // 2
    inverse = np.power(rope_base, -2.0 * np.arange(halfway) / rope_width).astype(np.float32)
    return np.concatenate([inverse, inverse])[None, :]


def cos_sin(angles):
    turns = jnp.floor(angles * np.float32(0.5 / np.pi) + 0.5)
    rest = ((angles - turns * turn_high) - turns * turn_middle) - turns * turn_low
    return jnp.cos(rest), jnp.sin(rest)


def pack(values, peak, total):
    def term(v):
        return v.astype(jnp.bfloat16).astype(jnp.float32)

    p0 = term(peak)
    p1 = term(peak - p0)
    p2 = peak - p0 - p1
    t0 = term(total)
    t1 = total - t0
    shape = peak.shape[:-1] + (tile,)
    lane = iota(shape, len(shape) - 1)
    stats = jnp.where(lane == 0, p0, jnp.where(lane == 1, p1, jnp.where(lane == 2, p2, jnp.where(lane == 3, t0, t1))))
    return values.astype(jnp.bfloat16), stats.astype(jnp.bfloat16)


def unpack(packed, width):
    values = packed[..., :width].astype(jnp.float32)
    stats = packed[..., width:].astype(jnp.float32)
    peak = stats[..., 0:1] + stats[..., 1:2] + stats[..., 2:3]
    total = stats[..., 3:4] + stats[..., 4:5]
    return values, peak, total


def merge(one, two):
    (va, pa, ta), (vb, pb, tb) = one, two
    peak = jnp.maximum(pa, pb)
    wa, wb = jnp.exp2(pa - peak), jnp.exp2(pb - peak)
    return va * wa + vb * wb, peak, ta * wa + tb * wb


def kernel(
    seq_size,
    lengths,
    positions,
    q_ref,
    new_ref,
    frequency_ref,
    up_keys_hbm,
    up_values_hbm,
    cache_hbm,
    out_ref,
    up_keys,
    up_values,
    cache,
    queries,
    new_keys,
    scores,
    partial,
    a_in,
    b_out,
    kept,
    b_in,
    c_out,
    c_in,
    gathered,
    load_sem,
    key_sem,
    value_sem,
    q1_send,
    q1_recv,
    qy_send,
    qy_recv,
    qf_send,
    qf_recv,
    a_send,
    a_recv,
    b_send,
    b_recv,
    c_send,
    c_recv,
    g_send,
    g_recv,
):
    steps, requests, heads, query_width = q_ref.shape
    nope, width = up_keys.shape[1], up_keys.shape[2]
    rope = query_width - nope
    rows_cached = cache.shape[2]
    rows = steps * heads
    piece = rows // owners
    all_rows = 4 * rows
    seq = lax.axis_index("seq")
    head = lax.axis_index("head")
    low = lax.rem(head, 2)
    high = lax.div(head, 2)
    near = head + 1 - 2 * low
    across = lax.rem(head + 2, 4)
    slot = seq * 4 + head
    owned = lax.rem(seq, owners)

    def at_head(h):
        return (seq, h)

    barrier = pltpu.get_barrier_semaphore()
    for h in (near, across):
        pl.semaphore_signal(barrier, inc=1, device_id=at_head(h), device_id_type=MESH)
    for d in range(1, seq_size):
        pl.semaphore_signal(barrier, inc=1, device_id=(lax.rem(seq + d, seq_size), head), device_id_type=MESH)

    key_load = pltpu.make_async_copy(up_keys_hbm, up_keys, key_sem)
    key_load.start()
    value_load = pltpu.make_async_copy(up_values_hbm.at[pl.ds(owned * 2, 2)], up_values, value_sem)

    def load(b):
        return pltpu.make_async_copy(cache_hbm.at[b], cache.at[b], load_sem.at[b])

    for b in range(requests):
        load(b).start()
    value_load.start()

    swap = (iota((rope, rope), 0) == lax.rem(iota((rope, rope), 1) + rope // 2, rope)).astype(jnp.bfloat16)
    grid_row = iota((steps * requests, rope), 0)
    grid = lax.div(grid_row, requests)
    for b in range(requests):
        grid = grid + jnp.where(lax.rem(grid_row, requests) == b, positions[b], 0)
    cosine, sine = cos_sin(grid.astype(jnp.float32) * frequency_ref[...])
    sine = jnp.where(iota((steps * requests, rope), 1) < rope // 2, -sine, sine)
    flat = q_ref[...].reshape(steps * requests * heads, query_width)
    q_rope = flat[:, nope:]
    swapped = jnp.dot(q_rope, swap, preferred_element_type=jnp.float32)
    three = (steps * requests, heads, rope)
    rotated = (
        q_rope.astype(jnp.float32).reshape(three) * cosine[:, None, :] + swapped.reshape(three) * sine[:, None, :]
    )
    rotated = rotated.astype(jnp.bfloat16).reshape(steps * requests * heads, rope)
    count = steps * requests * heads
    row = iota((count, count), 0)
    wanted = (row & (steps - 1)) * (requests * heads) + lax.div(row, rows) * heads + lax.div(lax.rem(row, rows), steps)
    order = (iota((count, count), 1) == wanted).astype(jnp.bfloat16)
    q_nope = jnp.dot(order, flat[:, :nope], preferred_element_type=jnp.float32).astype(jnp.bfloat16)
    rotated = jnp.dot(order, rotated, preferred_element_type=jnp.float32).astype(jnp.bfloat16)

    new_flat = new_ref[...].astype(jnp.float32).reshape(steps * requests, width + rope).astype(jnp.bfloat16)
    new_rope = new_flat[:, width:]
    new_swapped = jnp.dot(new_rope, swap, preferred_element_type=jnp.float32)
    new_rotated = new_rope.astype(jnp.float32) * cosine + new_swapped * sine
    new_keys[...] = jnp.zeros_like(new_keys)
    new_keys[: steps * requests, :width] = new_flat[:, :width]
    new_keys[: steps * requests, width:] = new_rotated.astype(jnp.bfloat16)

    own_head = lax.div(lax.rem(iota((count, nope), 0), rows), steps)
    spread = jnp.concatenate(
        [jnp.where(own_head == h, q_nope.astype(jnp.float32), 0.0).astype(jnp.bfloat16) for h in range(heads)], axis=1
    )
    key_load.wait()
    latent = jnp.dot(spread, up_keys[...].reshape(heads * nope, width), preferred_element_type=jnp.float32)
    latent = latent.astype(jnp.bfloat16)
    for b in range(requests):
        queries[b, head, :, :width] = latent[b * rows : (b + 1) * rows]
        queries[b, head, :, width:] = rotated[b * rows : (b + 1) * rows]

    def remote(source, target, send, recv, device):
        return pltpu.make_async_remote_copy(
            src_ref=source, dst_ref=target, send_sem=send, recv_sem=recv, device_id=device, device_id_type=MESH
        )

    def q_near(b):
        block = queries.at[b, head]
        return remote(block, block, q1_send.at[b], q1_recv.at[b], at_head(near))

    def q_across(b):
        block = queries.at[b, head]
        return remote(block, block, qy_send.at[b], qy_recv.at[b], at_head(across))

    def q_forward(b):
        block = queries.at[b, across]
        return remote(block, block, qf_send.at[b], qf_recv.at[b], at_head(near))

    def a_copy(b, j):
        return remote(
            partial.at[b, 1 - low + 2 * j], a_in.at[b, j], a_send.at[b, j], a_recv.at[b, j], at_head(near)
        )

    def b_copy(b):
        return remote(b_out.at[b], b_in.at[b], b_send.at[b], b_recv.at[b], at_head(across))

    def c_copy(p, target, source):
        return remote(
            c_out.at[p, target], c_in.at[p, source], c_send.at[p, target], c_recv.at[p, source], (target, head)
        )

    def g_copy(d):
        target = lax.rem(seq + d, seq_size)
        return remote(
            gathered.at[owned], gathered.at[owned], g_send.at[target], g_recv.at[owned], (target, head)
        )

    pl.semaphore_wait(barrier, 2 + seq_size - 1)
    for b in range(requests):
        q_across(b).start()
        q_near(b).start()

    q_across(0).wait_recv()
    q_forward(0).start()

    factor = log2_e * float(query_width) ** (-0.5)

    def attend(b):
        q_near(b).wait_recv()
        q_forward(b).wait_recv()
        load(b).wait()
        q = queries[b].reshape(all_rows, width + rope)
        length = lengths[b]
        peaks = jnp.full((all_rows, tile), lowest_peak, jnp.float32)

        def tiles(x, op, start):
            for i in range(x.shape[1] // tile):
                start = op(start, x[:, i * tile : (i + 1) * tile])
            return start

        nt = (((1,), (1,)), ((), ()))
        for c in range(rows_cached // chunk):
            s = jnp.dot(q, cache[b, :, c * chunk : (c + 1) * chunk], preferred_element_type=jnp.float32)
            number = slot * rows_cached + c * chunk + iota((1, chunk), 1)
            x = s * factor + jnp.where(number < length, 0.0, masked_score)
            scores[:, c * chunk : (c + 1) * chunk] = x
            peaks = tiles(x, jnp.maximum, peaks)
        s = lax.dot_general(q, new_keys[...], nt, preferred_element_type=jnp.float32)
        column = iota((all_rows, tile), 1)
        step = iota((all_rows, tile), 0) & (steps - 1)
        fresh = (
            (lax.rem(column, requests) == b)
            & (lax.div(column, requests) <= step)
            & (column < steps * requests)
            & (slot == 0)
        )
        x_new = s * factor + jnp.where(fresh, 0.0, masked_score)
        peak = jnp.max(jnp.maximum(peaks, x_new), axis=1, keepdims=True)

        @pl.when(b < requests - 1)
        def _():
            q_across(b + 1).wait_recv()
            q_forward(b + 1).start()

        weights = jnp.exp2(x_new - peak)
        totals = weights
        total_out = jnp.dot(weights.astype(jnp.bfloat16), new_keys[:, :width], preferred_element_type=jnp.float32)
        for c in range(rows_cached // chunk):
            weights = jnp.exp2(scores[:, c * chunk : (c + 1) * chunk] - peak)
            totals = tiles(weights, jnp.add, totals)
            total_out += lax.dot_general(
                weights.astype(jnp.bfloat16),
                cache[b, :width, c * chunk : (c + 1) * chunk],
                nt,
                preferred_element_type=jnp.float32,
            )
        total = jnp.sum(totals, axis=1, keepdims=True)
        values, stats = pack(total_out, peak, total)
        partial[b, :, :, :width] = values.reshape(4, rows, width)
        partial[b, :, :, width:] = stats.reshape(4, rows, tile)
        for j in range(2):
            a_copy(b, j).start()

    def merge_near(b):
        for j in range(2):
            a_copy(b, j).wait_recv()
        other = 1 - high
        merged = merge(
            unpack(partial[b, low + 2 * other], width),
            unpack(a_in[b, other], width),
        )
        values, stats = pack(*merged)
        b_out[b, :, :width] = values
        b_out[b, :, width:] = stats
        b_copy(b).start()
        values, peak, total = merge(
            unpack(partial[b, head], width),
            unpack(a_in[b, high], width),
        )
        kept[b, :, :width] = values
        kept[b, :, width:] = jnp.where(iota((rows, tile), 1) == 0, peak, total)

    def merge_across(b):
        b_copy(b).wait_recv()
        mine = (kept[b, :, :width], kept[b, :, width : width + 1], kept[b, :, width + 1 : width + 2])
        values, peak, total = merge(mine, unpack(b_in[b], width))
        kept[b, :, :width] = values
        kept[b, :, width:] = jnp.where(iota((rows, tile), 1) == 0, peak, total)

    def send_pair(p):
        both = jnp.concatenate(
            [kept[2 * p + i].reshape(owners, piece, width + tile) for i in range(2)], axis=1
        )
        values, stats = pack(both[..., :width], both[..., width : width + 1], both[..., width + 1 : width + 2])
        c_out[p, :, :, :width] = values
        c_out[p, :, :, width:] = stats
        for d in range(0 if seq_size > owners else 1, owners):
            target = lax.rem(seq + d, owners)
            if d == 0:
                @pl.when(seq >= owners)
                def _():
                    c_copy(p, target, seq).start()
            else:
                c_copy(p, target, seq).start()

    def finish_pair(p):
        c_in[p, owned] = c_out[p, owned]
        for d in range(1, seq_size):
            c_copy(p, owned, lax.rem(seq + d, seq_size)).wait_recv()
        values, peaks, totals = unpack(c_in[p], width)
        peak = jnp.max(peaks, axis=0, keepdims=True)
        scale = jnp.exp2(peaks - peak)
        mixed = jnp.sum(values * scale, axis=0) / jnp.sum(totals * scale, axis=0)
        both = 2 * piece
        second = lax.rem(iota((both, width), 0), piece) >= steps
        wide = jnp.concatenate([jnp.where(second, 0.0, mixed), jnp.where(second, mixed, 0.0)], axis=1)
        w0 = wide.astype(jnp.bfloat16)
        rest = wide - w0.astype(jnp.float32)
        w1 = rest.astype(jnp.bfloat16)
        w2 = (rest - w1.astype(jnp.float32)).astype(jnp.bfloat16)
        matrix = up_values[...].reshape(2 * width, up_values.shape[2])
        result = sum(jnp.dot(w, matrix, preferred_element_type=jnp.float32) for w in (w2, w1, w0))
        gathered[owned, p * both : (p + 1) * both, :] = result.astype(jnp.bfloat16)

    def body(b, carry):
        attend(b)

        @pl.when(b >= 1)
        def _():
            merge_near(b - 1)

        @pl.when(b >= 2)
        def _():
            merge_across(b - 2)

        @pl.when(b == requests - 1)
        def _():
            send_pair(0)

        return carry

    lax.fori_loop(0, requests, body, 0)
    merge_near(requests - 1)
    merge_across(requests - 2)
    value_load.wait()

    def when_owner(fn):
        if seq_size > owners:
            pl.when(seq < owners)(fn)
        else:
            fn()

    when_owner(lambda: finish_pair(0))
    merge_across(requests - 1)
    send_pair(1)

    def last():
        finish_pair(1)
        for d in range(1, seq_size):
            g_copy(d).start()

    when_owner(last)

    def from_owner(j):
        block = gathered.at[j]
        return remote(block, block, g_send.at[j], g_recv.at[j], (seq, near))

    for d in range(0 if seq_size > owners else 1, owners):
        source = lax.rem(seq + d, owners)
        if d == 0:
            @pl.when(seq >= owners)
            def _():
                from_owner(source).wait_recv()
        else:
            from_owner(source).wait_recv()

    per = rows * requests // owners
    row = iota((count, count), 0)
    s_of = lax.div(row, requests * heads)
    b_of = lax.rem(lax.div(row, heads), requests)
    h_of = lax.rem(row, heads)
    source = (
        lax.div(h_of, 2) * per + lax.div(b_of, 2) * (2 * piece) + (b_of & 1) * piece + (h_of & 1) * steps + s_of
    )
    back = (iota((count, count), 1) == source).astype(jnp.bfloat16)
    result = jnp.dot(back, gathered[...].reshape(count, -1), preferred_element_type=jnp.float32)
    out_ref[...] = result.astype(jnp.bfloat16).reshape(out_ref.shape)

    for b in range(requests):
        q_near(b).wait_send()
        q_across(b).wait_send()
        q_forward(b).wait_send()
        for j in range(2):
            a_copy(b, j).wait_send()
        b_copy(b).wait_send()
    for p in range(2):
        for d in range(0 if seq_size > owners else 1, owners):
            target = lax.rem(seq + d, owners)
            if d == 0:
                @pl.when(seq >= owners)
                def _():
                    c_copy(p, target, seq).wait_send()
            else:
                c_copy(p, target, seq).wait_send()

    def sent():
        for d in range(1, seq_size):
            g_copy(d).wait_send()

    when_owner(sent)


def on_device(seq_size, query_heads, up_keys, up_values, latent_cache, new_latent, context_lengths, positions):
    steps, requests, heads, query_width = query_heads.shape
    nope, width = up_keys.shape[1:]
    value_width = up_values.shape[2]
    key_width = latent_cache.shape[2]
    cached = latent_cache.shape[1]
    rows = steps * heads
    bf16, f32 = jnp.bfloat16, jnp.float32
    packed = width + tile
    dma = pltpu.SemaphoreType.DMA
    smem = pl.BlockSpec(memory_space=pltpu.SMEM)
    vmem = pl.BlockSpec(memory_space=pltpu.VMEM)
    anywhere = pl.BlockSpec(memory_space=pl.ANY)
    return pl.pallas_call(
        functools.partial(kernel, seq_size),
        out_shape=jax.ShapeDtypeStruct((steps, requests, heads, value_width), bf16),
        in_specs=[smem, smem, vmem, vmem, vmem, anywhere, anywhere, anywhere],
        out_specs=vmem,
        scratch_shapes=[
            pltpu.VMEM((heads, nope, width), bf16),
            pltpu.VMEM((2, width, value_width), bf16),
            pltpu.VMEM((requests, key_width, cached), bf16),
            pltpu.VMEM((requests, 4, rows, key_width), bf16),
            pltpu.VMEM((tile, key_width), bf16),
            pltpu.VMEM((4 * rows, cached), f32),
            pltpu.VMEM((requests, 4, rows, packed), bf16),
            pltpu.VMEM((requests, 2, rows, packed), bf16),
            pltpu.VMEM((requests, rows, packed), bf16),
            pltpu.VMEM((requests, rows, packed), f32),
            pltpu.VMEM((requests, rows, packed), bf16),
            pltpu.VMEM((2, owners, 2 * rows // owners, packed), bf16),
            pltpu.VMEM((2, seq_size, 2 * rows // owners, packed), bf16),
            pltpu.VMEM((owners, requests * rows // owners, value_width), bf16),
            dma((requests,)),
            dma,
            dma,
        ]
        + [dma((requests,))] * 6
        + [dma((requests, 2))] * 2
        + [dma((requests,))] * 2
        + [dma((2, owners)), dma((2, seq_size)), dma((seq_size,)), dma((owners,))],
        compiler_params=pltpu.CompilerParams(
            collective_id=0, has_side_effects=True, vmem_limit_bytes=56 * 1024 * 1024
        ),
        cost_estimate=pl.CostEstimate(
            flops=2 * requests * 4 * rows * cached * (key_width + width),
            bytes_accessed=2 * requests * cached * key_width,
            transcendentals=requests * 4 * rows * cached,
        ),
    )(
        context_lengths,
        positions,
        query_heads,
        new_latent,
        jnp.asarray(frequencies(query_width - nope)),
        up_keys,
        up_values,
        jnp.swapaxes(latent_cache, 1, 2),
    )


def solution(mesh):
    in_specs = (
        P(None, None, "head", None),
        P("head", None, None),
        P("head", None, None),
        P(None, ("seq", "head"), None),
        P(),
        P(),
        P(),
    )
    out_specs = P(None, None, "head", None)
    return jax.shard_map(
        functools.partial(on_device, mesh.shape["seq"]),
        mesh=mesh,
        in_specs=in_specs,
        out_specs=out_specs,
        check_vma=False,
    )
```

```python
import functools

import jax
import jax.numpy as jnp
import numpy as np
from jax import lax
from jax.experimental import pallas as pl
from jax.experimental.pallas import tpu as pltpu
from jax.sharding import PartitionSpec as P

MESH = pl.DeviceIdType.MESH
rope_base = 50000.0
masked_score = -1e30
lowest_peak = -1e29
log2_e = 1.4426950408889634
owners = 8
tile = 128
chunk = 512
turn_high = np.float32(6.28125)
turn_middle = np.float32(254 / 128 / 1024)
turn_low = np.float32(2 * np.pi - 6.28125 - 254 / 128 / 1024)


def iota(shape, axis):
    return lax.broadcasted_iota(jnp.int32, shape, axis)


def frequencies(rope_width):
    halfway = rope_width // 2
    inverse = np.power(rope_base, -2.0 * np.arange(halfway) / rope_width).astype(np.float32)
    return np.concatenate([inverse, inverse])[None, :]


def cos_sin(angles):
    turns = jnp.floor(angles * np.float32(0.5 / np.pi) + 0.5)
    rest = ((angles - turns * turn_high) - turns * turn_middle) - turns * turn_low
    return jnp.cos(rest), jnp.sin(rest)


def pack(values, peak, total):
    def term(v):
        return v.astype(jnp.bfloat16).astype(jnp.float32)

    p0 = term(peak)
    p1 = term(peak - p0)
    p2 = peak - p0 - p1
    t0 = term(total)
    t1 = total - t0
    shape = peak.shape[:-1] + (tile,)
    lane = iota(shape, len(shape) - 1)
    stats = jnp.where(lane == 0, p0, jnp.where(lane == 1, p1, jnp.where(lane == 2, p2, jnp.where(lane == 3, t0, t1))))
    return values.astype(jnp.bfloat16), stats.astype(jnp.bfloat16)


def unpack(packed, width):
    values = packed[..., :width].astype(jnp.float32)
    stats = packed[..., width:].astype(jnp.float32)
    peak = stats[..., 0:1] + stats[..., 1:2] + stats[..., 2:3]
    total = stats[..., 3:4] + stats[..., 4:5]
    return values, peak, total


def merge(one, two):
    (va, pa, ta), (vb, pb, tb) = one, two
    peak = jnp.maximum(pa, pb)
    wa, wb = jnp.exp2(pa - peak), jnp.exp2(pb - peak)
    return va * wa + vb * wb, peak, ta * wa + tb * wb


def kernel(
    seq_size,
    lengths,
    positions,
    q_ref,
    new_ref,
    frequency_ref,
    up_keys_hbm,
    up_values_hbm,
    cache_hbm,
    out_ref,
    up_keys,
    up_values,
    cache,
    queries,
    new_keys,
    scores,
    weights,
    partial,
    a_in,
    b_out,
    kept,
    b_in,
    c_out,
    c_in,
    mixed_latent,
    gathered,
    load_sem,
    key_sem,
    value_sem,
    q1_send,
    q1_recv,
    qy_send,
    qy_recv,
    qf_send,
    qf_recv,
    a_send,
    a_recv,
    b_send,
    b_recv,
    c_send,
    c_recv,
    g_send,
    g_recv,
):
    steps, requests, heads, query_width = q_ref.shape
    nope, width = up_keys.shape[1], up_keys.shape[2]
    rope = query_width - nope
    rows_cached = cache.shape[2]
    rows = steps * heads
    piece = rows // owners
    half = width // 2
    all_rows = 4 * rows
    seq = lax.axis_index("seq")
    head = lax.axis_index("head")
    low = lax.rem(head, 2)
    high = lax.div(head, 2)
    near = head + 1 - 2 * low
    across = lax.rem(head + 2, 4)
    slot = seq * 4 + head
    owned = lax.rem(seq, owners)

    def at_head(h):
        return (seq, h)

    barrier = pltpu.get_barrier_semaphore()
    for h in (near, across):
        pl.semaphore_signal(barrier, inc=1, device_id=at_head(h), device_id_type=MESH)
    for d in range(1, seq_size):
        pl.semaphore_signal(barrier, inc=1, device_id=(lax.rem(seq + d, seq_size), head), device_id_type=MESH)

    key_load = pltpu.make_async_copy(up_keys_hbm, up_keys, key_sem)
    key_load.start()
    value_load = pltpu.make_async_copy(up_values_hbm.at[pl.ds(owned * 2, 2)], up_values, value_sem)

    def load(b):
        return pltpu.make_async_copy(cache_hbm.at[b], cache.at[b, pl.ds(0, width + rope)], load_sem.at[b])

    swap = (iota((rope, rope), 0) == lax.rem(iota((rope, rope), 1) + rope // 2, rope)).astype(jnp.bfloat16)
    grid_row = iota((steps * requests, rope), 0)
    grid = lax.div(grid_row, requests)
    for b in range(requests):
        grid = grid + jnp.where(lax.rem(grid_row, requests) == b, positions[b], 0)
    cosine, sine = cos_sin(grid.astype(jnp.float32) * frequency_ref[...])
    sine = jnp.where(iota((steps * requests, rope), 1) < rope // 2, -sine, sine)
    flat = q_ref[...].reshape(steps * requests * heads, query_width)
    q_rope = flat[:, nope:]
    swapped = jnp.dot(q_rope, swap, preferred_element_type=jnp.float32)
    three = (steps * requests, heads, rope)
    rotated = (
        q_rope.astype(jnp.float32).reshape(three) * cosine[:, None, :] + swapped.reshape(three) * sine[:, None, :]
    )
    rotated = rotated.astype(jnp.bfloat16).reshape(steps * requests * heads, rope)
    rotated = jnp.concatenate([rotated, jnp.zeros_like(rotated)], axis=1)
    count = steps * requests * heads
    row = iota((count, count), 0)
    wanted = (row & (steps - 1)) * (requests * heads) + lax.div(row, rows) * heads + lax.div(lax.rem(row, rows), steps)
    order = (iota((count, count), 1) == wanted).astype(jnp.bfloat16)
    q_nope = jnp.dot(order, flat[:, :nope], preferred_element_type=jnp.float32).astype(jnp.bfloat16)
    rotated = jnp.dot(order, rotated, preferred_element_type=jnp.float32).astype(jnp.bfloat16)

    new_flat = new_ref[...].astype(jnp.float32).reshape(steps * requests, width + rope).astype(jnp.bfloat16)
    new_rope = new_flat[:, width:]
    new_swapped = jnp.dot(new_rope, swap, preferred_element_type=jnp.float32)
    new_rotated = new_rope.astype(jnp.float32) * cosine + new_swapped * sine
    new_keys[...] = jnp.zeros_like(new_keys)
    new_keys[: steps * requests, :width] = new_flat[:, :width]
    new_keys[: steps * requests, width : width + rope] = new_rotated.astype(jnp.bfloat16)

    own_head = lax.div(lax.rem(iota((count, nope), 0), rows), steps)
    spread = jnp.concatenate(
        [jnp.where(own_head == h, q_nope.astype(jnp.float32), 0.0).astype(jnp.bfloat16) for h in range(heads)], axis=1
    )
    key_load.wait()
    for b in range(requests):
        load(b).start()
    value_load.start()
    latent = jnp.dot(spread, up_keys[...].reshape(heads * nope, width), preferred_element_type=jnp.float32)
    latent = latent.astype(jnp.bfloat16)
    for b in range(requests):
        queries[b, head, :, :width] = latent[b * rows : (b + 1) * rows]
        queries[b, head, :, width : width + tile] = rotated[b * rows : (b + 1) * rows]
        cache[b, width + rope :, :] = jnp.zeros((tile - rope, rows_cached), jnp.bfloat16)

    def remote(source, target, send, recv, device):
        return pltpu.make_async_remote_copy(
            src_ref=source, dst_ref=target, send_sem=send, recv_sem=recv, device_id=device, device_id_type=MESH
        )

    def q_near(b):
        block = queries.at[b, head]
        return remote(block, block, q1_send.at[b], q1_recv.at[b], at_head(near))

    def q_across(b):
        block = queries.at[b, head]
        return remote(block, block, qy_send.at[b], qy_recv.at[b], at_head(across))

    def q_forward(b):
        block = queries.at[b, across]
        return remote(block, block, qf_send.at[b], qf_recv.at[b], at_head(near))

    def a_copy(b, j):
        return remote(
            partial.at[b, 1 - low + 2 * j], a_in.at[b, j], a_send.at[b, j], a_recv.at[b, j], at_head(near)
        )

    def b_copy(b):
        return remote(b_out.at[b], b_in.at[b], b_send.at[b], b_recv.at[b], at_head(across))

    def c_copy(p, target, source):
        return remote(
            c_out.at[p, target], c_in.at[p, source], c_send.at[p, target], c_recv.at[p, source], (target, head)
        )

    def g_copy(d):
        target = lax.rem(seq + d, seq_size)
        return remote(
            gathered.at[owned], gathered.at[owned], g_send.at[target], g_recv.at[owned], (target, head)
        )

    pl.semaphore_wait(barrier, 2 + seq_size - 1)
    for b in range(requests):
        q_across(b).start()
        q_near(b).start()

    factor = log2_e * float(query_width) ** (-0.5)
    nt = (((1,), (1,)), ((), ()))
    spans = [slice(c * chunk, (c + 1) * chunk) for c in range(rows_cached // chunk)]

    def tiles(x, op, start):
        for i in range(x.shape[1] // tile):
            start = op(start, x[:, i * tile : (i + 1) * tile])
        return start

    def forward(b):
        q_across(b).wait_recv()
        q_forward(b).start()

    def ready(b):
        q_near(b).wait_recv()
        q_forward(b).wait_recv()
        load(b).wait()

    def score(b, span, peaks):
        q = queries[b].reshape(all_rows, width + tile)
        s = jnp.dot(q, cache[b, :, span], preferred_element_type=jnp.float32)
        number = slot * rows_cached + span.start + iota((1, chunk), 1)
        x = s * factor + jnp.where(number < lengths[b], 0.0, masked_score)
        scores[b % 2, :, span] = x
        return tiles(x, jnp.maximum, peaks)

    def score_new(b, peaks):
        q = queries[b].reshape(all_rows, width + tile)
        s = lax.dot_general(q, new_keys[...], nt, preferred_element_type=jnp.float32)
        column = iota((all_rows, tile), 1)
        step = iota((all_rows, tile), 0) & (steps - 1)
        fresh = (
            (lax.rem(column, requests) == b)
            & (lax.div(column, requests) <= step)
            & (column < steps * requests)
            & (slot == 0)
        )
        x = s * factor + jnp.where(fresh, 0.0, masked_score)
        return x, jnp.max(jnp.maximum(peaks, x), axis=1, keepdims=True)

    lowest = jnp.full((all_rows, tile), lowest_peak, jnp.float32)

    def attend(b, x_new, peak):
        more = b + 1 < requests
        peaks = lowest
        fresh = jnp.exp2(x_new - peak)
        totals = fresh
        for span in spans:
            if more:
                peaks = score(b + 1, span, peaks)
            w = jnp.exp2(scores[b % 2, :, span] - peak)
            totals = tiles(w, jnp.add, totals)
            weights[:, span] = w.astype(jnp.bfloat16)
        following = score_new(b + 1, peaks) if more else None
        mixed = jnp.dot(fresh.astype(jnp.bfloat16), new_keys[:, :width], preferred_element_type=jnp.float32)
        mixed += lax.dot_general(weights[...], cache[b, :width, :], nt, preferred_element_type=jnp.float32)
        values, stats = pack(mixed, peak, jnp.sum(totals, axis=1, keepdims=True))
        partial[b, :, :, :width] = values.reshape(4, rows, width)
        partial[b, :, :, width:] = stats.reshape(4, rows, tile)
        for j in range(2):
            a_copy(b, j).start()
        return following

    def merge_near(b):
        for j in range(2):
            a_copy(b, j).wait_recv()
        other = 1 - high
        merged = merge(
            unpack(partial[b, low + 2 * other], width),
            unpack(a_in[b, other], width),
        )
        values, stats = pack(*merged)
        b_out[b, :, :width] = values
        b_out[b, :, width:] = stats
        b_copy(b).start()
        values, peak, total = merge(
            unpack(partial[b, head], width),
            unpack(a_in[b, high], width),
        )
        kept[b, :, :width] = values
        kept[b, :, width:] = jnp.where(iota((rows, tile), 1) == 0, peak, total)

    def merge_across(b):
        b_copy(b).wait_recv()
        mine = (kept[b, :, :width], kept[b, :, width : width + 1], kept[b, :, width + 1 : width + 2])
        values, stats = pack(*merge(mine, unpack(b_in[b], width)))
        values = values.astype(jnp.float32).reshape(owners, piece, width)
        stats = stats.astype(jnp.float32).reshape(owners, piece, tile)
        c_out[b, :, :, :half] = jnp.concatenate([values[..., :half], values[..., half:]], axis=1).astype(jnp.bfloat16)
        c_out[b, :, :, half:] = jnp.concatenate([stats, stats], axis=1).astype(jnp.bfloat16)
        for d in range(0 if seq_size > owners else 1, owners):
            target = lax.rem(seq + d, owners)
            if d == 0:
                @pl.when(seq >= owners)
                def _():
                    c_copy(b, target, seq).start()
            else:
                c_copy(b, target, seq).start()

    def when_owner(fn):
        if seq_size > owners:
            pl.when(seq < owners)(fn)
        else:
            fn()

    def finish(b):
        def combine():
            c_in[b, owned] = c_out[b, owned]
            for d in range(1, seq_size):
                c_copy(b, owned, lax.rem(seq + d, seq_size)).wait_recv()
            values, peaks, totals = unpack(c_in[b], half)
            peak = jnp.max(peaks, axis=0, keepdims=True)
            scale = jnp.exp2(peaks - peak)
            mixed = jnp.sum(values * scale, axis=0) / jnp.sum(totals * scale, axis=0)
            mixed_latent[b, :, :half] = mixed[:piece]
            mixed_latent[b, :, half:] = mixed[piece:]

        when_owner(combine)

    def project():
        mixed = mixed_latent[...].reshape(requests * piece, width)
        second = lax.rem(iota(mixed.shape, 0), piece) >= steps
        wide = jnp.concatenate([jnp.where(second, 0.0, mixed), jnp.where(second, mixed, 0.0)], axis=1)
        w0 = wide.astype(jnp.bfloat16)
        rest = wide - w0.astype(jnp.float32)
        w1 = rest.astype(jnp.bfloat16)
        w2 = (rest - w1.astype(jnp.float32)).astype(jnp.bfloat16)
        matrix = up_values[...].reshape(2 * width, up_values.shape[2])
        result = sum(jnp.dot(w, matrix, preferred_element_type=jnp.float32) for w in (w2, w1, w0))
        gathered[owned] = result.astype(jnp.bfloat16)

    forward(0)
    forward(1)
    ready(0)
    peaks = lowest
    for span in spans:
        peaks = score(0, span, peaks)
    following = score_new(0, peaks)
    for b in range(requests):
        if b + 2 < requests:
            forward(b + 2)
        if b + 1 < requests:
            ready(b + 1)
        following = attend(b, *following)
        if b >= 1:
            merge_near(b - 1)
        if b >= 2:
            merge_across(b - 2)
        if b >= 3:
            finish(b - 3)
    merge_near(requests - 1)
    merge_across(requests - 2)
    finish(requests - 3)
    value_load.wait()
    merge_across(requests - 1)
    finish(requests - 2)
    finish(requests - 1)

    def last():
        project()
        for d in range(1, seq_size):
            g_copy(d).start()

    when_owner(last)

    def from_owner(j):
        block = gathered.at[j]
        return remote(block, block, g_send.at[j], g_recv.at[j], (seq, near))

    for d in range(0 if seq_size > owners else 1, owners):
        source = lax.rem(seq + d, owners)
        if d == 0:
            @pl.when(seq >= owners)
            def _():
                from_owner(source).wait_recv()
        else:
            from_owner(source).wait_recv()

    per = rows * requests // owners
    row = iota((count, count), 0)
    s_of = lax.div(row, requests * heads)
    b_of = lax.rem(lax.div(row, heads), requests)
    h_of = lax.rem(row, heads)
    source = lax.div(h_of, 2) * per + b_of * piece + (h_of & 1) * steps + s_of
    back = (iota((count, count), 1) == source).astype(jnp.bfloat16)
    result = jnp.dot(back, gathered[...].reshape(count, -1), preferred_element_type=jnp.float32)
    out_ref[...] = result.reshape(out_ref.shape)

    for b in range(requests):
        q_near(b).wait_send()
        q_across(b).wait_send()
        q_forward(b).wait_send()
        for j in range(2):
            a_copy(b, j).wait_send()
        b_copy(b).wait_send()
    for p in range(requests):
        for d in range(0 if seq_size > owners else 1, owners):
            target = lax.rem(seq + d, owners)
            if d == 0:
                @pl.when(seq >= owners)
                def _():
                    c_copy(p, target, seq).wait_send()
            else:
                c_copy(p, target, seq).wait_send()

    def sent():
        for d in range(1, seq_size):
            g_copy(d).wait_send()

    when_owner(sent)


def on_device(seq_size, query_heads, up_keys, up_values, latent_cache, new_latent, context_lengths, positions):
    steps, requests, heads, query_width = query_heads.shape
    nope, width = up_keys.shape[1:]
    value_width = up_values.shape[2]
    key_width = latent_cache.shape[2]
    cached = latent_cache.shape[1]
    rows = steps * heads
    bf16, f32 = jnp.bfloat16, jnp.float32
    packed = width + tile
    dma = pltpu.SemaphoreType.DMA
    smem = pl.BlockSpec(memory_space=pltpu.SMEM)
    vmem = pl.BlockSpec(memory_space=pltpu.VMEM)
    anywhere = pl.BlockSpec(memory_space=pl.ANY)
    attended = pl.pallas_call(
        functools.partial(kernel, seq_size),
        out_shape=jax.ShapeDtypeStruct((steps, requests, heads, value_width), f32),
        in_specs=[smem, smem, vmem, vmem, vmem, anywhere, anywhere, anywhere],
        out_specs=vmem,
        scratch_shapes=[
            pltpu.VMEM((heads, nope, width), bf16),
            pltpu.VMEM((2, width, value_width), bf16),
            pltpu.VMEM((requests, packed, cached), bf16),
            pltpu.VMEM((requests, 4, rows, packed), bf16),
            pltpu.VMEM((tile, packed), bf16),
            pltpu.VMEM((2, 4 * rows, cached), f32),
            pltpu.VMEM((4 * rows, cached), bf16),
            pltpu.VMEM((requests, 4, rows, packed), bf16),
            pltpu.VMEM((requests, 2, rows, packed), bf16),
            pltpu.VMEM((requests, rows, packed), bf16),
            pltpu.VMEM((requests, rows, packed), f32),
            pltpu.VMEM((requests, rows, packed), bf16),
            pltpu.VMEM((requests, owners, 2 * rows // owners, width // 2 + tile), bf16),
            pltpu.VMEM((requests, seq_size, 2 * rows // owners, width // 2 + tile), bf16),
            pltpu.VMEM((requests, rows // owners, width), f32),
            pltpu.VMEM((owners, requests * rows // owners, value_width), bf16),
            dma((requests,)),
            dma,
            dma,
        ]
        + [dma((requests,))] * 6
        + [dma((requests, 2))] * 2
        + [dma((requests,))] * 2
        + [dma((requests, owners)), dma((requests, seq_size)), dma((seq_size,)), dma((owners,))],
        compiler_params=pltpu.CompilerParams(
            collective_id=0, has_side_effects=True, vmem_limit_bytes=56 * 1024 * 1024
        ),
        cost_estimate=pl.CostEstimate(
            flops=2 * requests * 4 * rows * cached * (key_width + width),
            bytes_accessed=2 * requests * cached * key_width,
            transcendentals=requests * 4 * rows * cached,
        ),
    )(
        context_lengths,
        positions,
        query_heads,
        new_latent,
        jnp.asarray(frequencies(query_width - nope)),
        up_keys,
        up_values,
        jnp.swapaxes(latent_cache, 1, 2),
    )
    return attended.astype(bf16)


def solution(mesh):
    in_specs = (
        P(None, None, "head", None),
        P("head", None, None),
        P("head", None, None),
        P(None, ("seq", "head"), None),
        P(),
        P(),
        P(),
    )
    out_specs = P(None, None, "head", None)
    return jax.shard_map(
        functools.partial(on_device, mesh.shape["seq"]),
        mesh=mesh,
        in_specs=in_specs,
        out_specs=out_specs,
        check_vma=False,
    )
```

```python
import functools

import jax
import jax.numpy as jnp
import numpy as np
from jax import lax
from jax.experimental import pallas as pl
from jax.experimental.pallas import tpu as pltpu
from jax.sharding import PartitionSpec as P

MESH = pl.DeviceIdType.MESH
rope_base = 50000.0
masked_score = -1e30
lowest_peak = -1e29
log2_e = 1.4426950408889634
owners = 8
tile = 128
chunk = 512
turn_high = np.float32(6.28125)
turn_middle = np.float32(254 / 128 / 1024)
turn_low = np.float32(2 * np.pi - 6.28125 - 254 / 128 / 1024)


def iota(shape, axis):
    return lax.broadcasted_iota(jnp.int32, shape, axis)


def frequencies(rope_width):
    halfway = rope_width // 2
    inverse = np.power(rope_base, -2.0 * np.arange(halfway) / rope_width).astype(np.float32)
    return np.concatenate([inverse, inverse])[None, :]


def cos_sin(angles):
    turns = jnp.floor(angles * np.float32(0.5 / np.pi) + 0.5)
    rest = ((angles - turns * turn_high) - turns * turn_middle) - turns * turn_low
    return jnp.cos(rest), jnp.sin(rest)


def pack(values, peak, total):
    def term(v):
        return v.astype(jnp.bfloat16).astype(jnp.float32)

    p0 = term(peak)
    p1 = term(peak - p0)
    p2 = peak - p0 - p1
    t0 = term(total)
    t1 = total - t0
    shape = peak.shape[:-1] + (tile,)
    lane = iota(shape, len(shape) - 1)
    stats = jnp.where(lane == 0, p0, jnp.where(lane == 1, p1, jnp.where(lane == 2, p2, jnp.where(lane == 3, t0, t1))))
    return values.astype(jnp.bfloat16), stats.astype(jnp.bfloat16)


def unpack(packed, width):
    values = packed[..., :width].astype(jnp.float32)
    stats = packed[..., width:].astype(jnp.float32)
    peak = stats[..., 0:1] + stats[..., 1:2] + stats[..., 2:3]
    total = stats[..., 3:4] + stats[..., 4:5]
    return values, peak, total


def merge(one, two):
    (va, pa, ta), (vb, pb, tb) = one, two
    peak = jnp.maximum(pa, pb)
    wa, wb = jnp.exp2(pa - peak), jnp.exp2(pb - peak)
    return va * wa + vb * wb, peak, ta * wa + tb * wb


def kernel(
    seq_size,
    lengths,
    positions,
    q_hbm,
    new_hbm,
    frequency_ref,
    up_keys_hbm,
    up_values_hbm,
    cache_hbm,
    out_ref,
    q_ref,
    new_ref,
    up_keys,
    up_values,
    cache,
    queries,
    new_keys,
    scores,
    weights,
    partial,
    a_in,
    b_out,
    kept,
    b_in,
    c_out,
    c_in,
    mixed_latent,
    gathered,
    small_sem,
    load_sem,
    key_sem,
    value_sem,
    q1_send,
    q1_recv,
    qy_send,
    qy_recv,
    qf_send,
    qf_recv,
    a_send,
    a_recv,
    b_send,
    b_recv,
    c_send,
    c_recv,
    g_send,
    g_recv,
):
    steps, requests, heads, query_width = q_ref.shape
    nope, width = up_keys.shape[1], up_keys.shape[2]
    rope = query_width - nope
    rows_cached = cache.shape[2]
    rows = steps * heads
    piece = rows // owners
    half = width // 2
    all_rows = 4 * rows
    seq = lax.axis_index("seq")
    head = lax.axis_index("head")
    low = lax.rem(head, 2)
    high = lax.div(head, 2)
    near = head + 1 - 2 * low
    across = lax.rem(head + 2, 4)
    slot = seq * 4 + head
    owned = lax.rem(seq, owners)

    def at_head(h):
        return (seq, h)

    barrier = pltpu.get_barrier_semaphore()
    for h in (near, across):
        pl.semaphore_signal(barrier, inc=1, device_id=at_head(h), device_id_type=MESH)
    for d in range(1, seq_size):
        pl.semaphore_signal(barrier, inc=1, device_id=(lax.rem(seq + d, seq_size), head), device_id_type=MESH)

    key_load = pltpu.make_async_copy(up_keys_hbm, up_keys, key_sem)
    key_load.start()
    q_load = pltpu.make_async_copy(q_hbm, q_ref, small_sem.at[0])
    new_load = pltpu.make_async_copy(new_hbm, new_ref, small_sem.at[1])
    q_load.start()
    new_load.start()
    value_load = pltpu.make_async_copy(up_values_hbm.at[pl.ds(owned * 2, 2)], up_values, value_sem)

    def load(b):
        return pltpu.make_async_copy(cache_hbm.at[b], cache.at[b, pl.ds(0, width + rope)], load_sem.at[b])

    swap = (iota((rope, rope), 0) == lax.rem(iota((rope, rope), 1) + rope // 2, rope)).astype(jnp.bfloat16)
    grid_row = iota((steps * requests, rope), 0)
    grid = lax.div(grid_row, requests)
    for b in range(requests):
        grid = grid + jnp.where(lax.rem(grid_row, requests) == b, positions[b], 0)
    cosine, sine = cos_sin(grid.astype(jnp.float32) * frequency_ref[...])
    sine = jnp.where(iota((steps * requests, rope), 1) < rope // 2, -sine, sine)
    q_load.wait()
    flat = q_ref[...].reshape(steps * requests * heads, query_width)
    q_rope = flat[:, nope:]
    swapped = jnp.dot(q_rope, swap, preferred_element_type=jnp.float32)
    three = (steps * requests, heads, rope)
    rotated = (
        q_rope.astype(jnp.float32).reshape(three) * cosine[:, None, :] + swapped.reshape(three) * sine[:, None, :]
    )
    rotated = rotated.astype(jnp.bfloat16).reshape(steps * requests * heads, rope)
    rotated = jnp.concatenate([rotated, jnp.zeros_like(rotated)], axis=1)
    count = steps * requests * heads
    row = iota((count, count), 0)
    wanted = (row & (steps - 1)) * (requests * heads) + lax.div(row, rows) * heads + lax.div(lax.rem(row, rows), steps)
    order = (iota((count, count), 1) == wanted).astype(jnp.bfloat16)
    q_nope = jnp.dot(order, flat[:, :nope], preferred_element_type=jnp.float32).astype(jnp.bfloat16)
    rotated = jnp.dot(order, rotated, preferred_element_type=jnp.float32).astype(jnp.bfloat16)

    new_load.wait()
    new_flat = new_ref[...].astype(jnp.float32).reshape(steps * requests, width + rope).astype(jnp.bfloat16)
    new_rope = new_flat[:, width:]
    new_swapped = jnp.dot(new_rope, swap, preferred_element_type=jnp.float32)
    new_rotated = new_rope.astype(jnp.float32) * cosine + new_swapped * sine
    new_keys[...] = jnp.zeros_like(new_keys)
    new_keys[: steps * requests, :width] = new_flat[:, :width]
    new_keys[: steps * requests, width : width + rope] = new_rotated.astype(jnp.bfloat16)

    own_head = lax.div(lax.rem(iota((count, nope), 0), rows), steps)
    spread = jnp.concatenate(
        [jnp.where(own_head == h, q_nope.astype(jnp.float32), 0.0).astype(jnp.bfloat16) for h in range(heads)], axis=1
    )
    key_load.wait()
    for b in range(requests):
        load(b).start()
    value_load.start()
    latent = jnp.dot(spread, up_keys[...].reshape(heads * nope, width), preferred_element_type=jnp.float32)
    latent = latent.astype(jnp.bfloat16)
    for b in range(requests):
        queries[b, head, :, :width] = latent[b * rows : (b + 1) * rows]
        queries[b, head, :, width : width + tile] = rotated[b * rows : (b + 1) * rows]
        cache[b, width + rope :, :] = jnp.zeros((tile - rope, rows_cached), jnp.bfloat16)

    def remote(source, target, send, recv, device):
        return pltpu.make_async_remote_copy(
            src_ref=source, dst_ref=target, send_sem=send, recv_sem=recv, device_id=device, device_id_type=MESH
        )

    def q_near(b):
        block = queries.at[b, head]
        return remote(block, block, q1_send.at[b], q1_recv.at[b], at_head(near))

    def q_across(b):
        block = queries.at[b, head]
        return remote(block, block, qy_send.at[b], qy_recv.at[b], at_head(across))

    def q_forward(b):
        block = queries.at[b, across]
        return remote(block, block, qf_send.at[b], qf_recv.at[b], at_head(near))

    def a_copy(b, j):
        return remote(
            partial.at[b, 1 - low + 2 * j], a_in.at[b, j], a_send.at[b, j], a_recv.at[b, j], at_head(near)
        )

    def b_copy(b):
        return remote(b_out.at[b], b_in.at[b], b_send.at[b], b_recv.at[b], at_head(across))

    def c_copy(p, target, source):
        return remote(
            c_out.at[p, target], c_in.at[p, source], c_send.at[p, target], c_recv.at[p, source], (target, head)
        )

    def g_copy(d):
        target = lax.rem(seq + d, seq_size)
        return remote(
            gathered.at[owned], gathered.at[owned], g_send.at[target], g_recv.at[owned], (target, head)
        )

    pl.semaphore_wait(barrier, 2 + seq_size - 1)
    for b in range(requests):
        q_across(b).start()
        q_near(b).start()

    factor = log2_e * float(query_width) ** (-0.5)
    nt = (((1,), (1,)), ((), ()))
    spans = [slice(c * chunk, (c + 1) * chunk) for c in range(rows_cached // chunk)]

    def tiles(x, op, start):
        for i in range(x.shape[1] // tile):
            start = op(start, x[:, i * tile : (i + 1) * tile])
        return start

    def forward(b):
        q_across(b).wait_recv()
        q_forward(b).start()

    def ready(b):
        q_near(b).wait_recv()
        q_forward(b).wait_recv()
        load(b).wait()

    def score(b, span, peaks):
        q = queries[b].reshape(all_rows, width + tile)
        s = jnp.dot(q, cache[b, :, span], preferred_element_type=jnp.float32)
        number = slot * rows_cached + span.start + iota((1, chunk), 1)
        x = s * factor + jnp.where(number < lengths[b], 0.0, masked_score)
        scores[b % 2, :, span] = x
        return tiles(x, jnp.maximum, peaks)

    def score_new(b, peaks):
        q = queries[b].reshape(all_rows, width + tile)
        s = lax.dot_general(q, new_keys[...], nt, preferred_element_type=jnp.float32)
        column = iota((all_rows, tile), 1)
        step = iota((all_rows, tile), 0) & (steps - 1)
        fresh = (
            (lax.rem(column, requests) == b)
            & (lax.div(column, requests) <= step)
            & (column < steps * requests)
            & (slot == 0)
        )
        x = s * factor + jnp.where(fresh, 0.0, masked_score)
        return x, jnp.max(jnp.maximum(peaks, x), axis=1, keepdims=True)

    lowest = jnp.full((all_rows, tile), lowest_peak, jnp.float32)

    def attend(b, x_new, peak):
        more = b + 1 < requests
        peaks = lowest
        fresh = jnp.exp2(x_new - peak)
        totals = fresh
        for place, span in enumerate(spans):
            if more:
                peaks = score(b + 1, span, peaks)
            w = jnp.exp2(scores[b % 2, :, span] - peak)
            totals = tiles(w, jnp.add, totals)
            weights[:, span] = w.astype(jnp.bfloat16)
            if place == len(spans) // 2 and b >= 1:
                merge_near(b - 1)
        if b >= 2:
            merge_across(b - 2)
        if b >= 3:
            finish(b - 3)
        following = score_new(b + 1, peaks) if more else None
        mixed = jnp.dot(fresh.astype(jnp.bfloat16), new_keys[:, :width], preferred_element_type=jnp.float32)
        mixed += lax.dot_general(weights[...], cache[b, :width, :], nt, preferred_element_type=jnp.float32)
        values, stats = pack(mixed, peak, jnp.sum(totals, axis=1, keepdims=True))
        partial[b, :, :, :width] = values.reshape(4, rows, width)
        partial[b, :, :, width:] = stats.reshape(4, rows, tile)
        for j in range(2):
            a_copy(b, j).start()
        return following

    def merge_near(b):
        for j in range(2):
            a_copy(b, j).wait_recv()
        other = 1 - high
        merged = merge(
            unpack(partial[b, low + 2 * other], width),
            unpack(a_in[b, other], width),
        )
        values, stats = pack(*merged)
        b_out[b, :, :width] = values
        b_out[b, :, width:] = stats
        b_copy(b).start()
        values, peak, total = merge(
            unpack(partial[b, head], width),
            unpack(a_in[b, high], width),
        )
        kept[b, :, :width] = values
        kept[b, :, width:] = jnp.where(iota((rows, tile), 1) == 0, peak, total)

    def merge_across(b):
        b_copy(b).wait_recv()
        mine = (kept[b, :, :width], kept[b, :, width : width + 1], kept[b, :, width + 1 : width + 2])
        values, stats = pack(*merge(mine, unpack(b_in[b], width)))
        values = values.astype(jnp.float32).reshape(owners, piece, width)
        stats = stats.astype(jnp.float32).reshape(owners, piece, tile)
        c_out[b, :, :, :half] = jnp.concatenate([values[..., :half], values[..., half:]], axis=1).astype(jnp.bfloat16)
        c_out[b, :, :, half:] = jnp.concatenate([stats, stats], axis=1).astype(jnp.bfloat16)
        for d in range(0 if seq_size > owners else 1, owners):
            target = lax.rem(seq + d, owners)
            if d == 0:
                @pl.when(seq >= owners)
                def _():
                    c_copy(b, target, seq).start()
            else:
                c_copy(b, target, seq).start()

    def when_owner(fn):
        if seq_size > owners:
            pl.when(seq < owners)(fn)
        else:
            fn()

    def finish(b):
        def combine():
            c_in[b, owned] = c_out[b, owned]
            for d in range(1, seq_size):
                c_copy(b, owned, lax.rem(seq + d, seq_size)).wait_recv()
            values, peaks, totals = unpack(c_in[b], half)
            peak = jnp.max(peaks, axis=0, keepdims=True)
            scale = jnp.exp2(peaks - peak)
            mixed = jnp.sum(values * scale, axis=0) / jnp.sum(totals * scale, axis=0)
            mixed_latent[b, :, :half] = mixed[:piece]
            mixed_latent[b, :, half:] = mixed[piece:]

        when_owner(combine)

    def project():
        mixed = mixed_latent[...].reshape(requests * piece, width)
        second = lax.rem(iota(mixed.shape, 0), piece) >= steps
        wide = jnp.concatenate([jnp.where(second, 0.0, mixed), jnp.where(second, mixed, 0.0)], axis=1)
        w0 = wide.astype(jnp.bfloat16)
        rest = wide - w0.astype(jnp.float32)
        w1 = rest.astype(jnp.bfloat16)
        w2 = (rest - w1.astype(jnp.float32)).astype(jnp.bfloat16)
        matrix = up_values[...].reshape(2 * width, up_values.shape[2])
        result = sum(jnp.dot(w, matrix, preferred_element_type=jnp.float32) for w in (w2, w1, w0))
        gathered[owned] = result.astype(jnp.bfloat16)

    forward(0)
    forward(1)
    ready(0)
    peaks = lowest
    for span in spans:
        peaks = score(0, span, peaks)
    following = score_new(0, peaks)
    for b in range(requests):
        if b + 2 < requests:
            forward(b + 2)
        if b + 1 < requests:
            ready(b + 1)
        following = attend(b, *following)
    merge_near(requests - 1)
    merge_across(requests - 2)
    finish(requests - 3)
    value_load.wait()
    merge_across(requests - 1)
    finish(requests - 2)
    finish(requests - 1)

    def last():
        project()
        for d in range(1, seq_size):
            g_copy(d).start()

    when_owner(last)

    def from_owner(j):
        block = gathered.at[j]
        return remote(block, block, g_send.at[j], g_recv.at[j], (seq, near))

    for d in range(0 if seq_size > owners else 1, owners):
        source = lax.rem(seq + d, owners)
        if d == 0:
            @pl.when(seq >= owners)
            def _():
                from_owner(source).wait_recv()
        else:
            from_owner(source).wait_recv()

    per = rows * requests // owners
    row = iota((count, count), 0)
    s_of = lax.div(row, requests * heads)
    b_of = lax.rem(lax.div(row, heads), requests)
    h_of = lax.rem(row, heads)
    source = lax.div(h_of, 2) * per + b_of * piece + (h_of & 1) * steps + s_of
    back = (iota((count, count), 1) == source).astype(jnp.bfloat16)
    result = jnp.dot(back, gathered[...].reshape(count, -1), preferred_element_type=jnp.float32)
    out_ref[...] = result.reshape(out_ref.shape)

    for b in range(requests):
        q_near(b).wait_send()
        q_across(b).wait_send()
        q_forward(b).wait_send()
        for j in range(2):
            a_copy(b, j).wait_send()
        b_copy(b).wait_send()
    for p in range(requests):
        for d in range(0 if seq_size > owners else 1, owners):
            target = lax.rem(seq + d, owners)
            if d == 0:
                @pl.when(seq >= owners)
                def _():
                    c_copy(p, target, seq).wait_send()
            else:
                c_copy(p, target, seq).wait_send()

    def sent():
        for d in range(1, seq_size):
            g_copy(d).wait_send()

    when_owner(sent)


def on_device(seq_size, query_heads, up_keys, up_values, latent_cache, new_latent, context_lengths, positions):
    steps, requests, heads, query_width = query_heads.shape
    nope, width = up_keys.shape[1:]
    value_width = up_values.shape[2]
    key_width = latent_cache.shape[2]
    cached = latent_cache.shape[1]
    rows = steps * heads
    bf16, f32 = jnp.bfloat16, jnp.float32
    packed = width + tile
    dma = pltpu.SemaphoreType.DMA
    smem = pl.BlockSpec(memory_space=pltpu.SMEM)
    vmem = pl.BlockSpec(memory_space=pltpu.VMEM)
    anywhere = pl.BlockSpec(memory_space=pl.ANY)
    attended = pl.pallas_call(
        functools.partial(kernel, seq_size),
        out_shape=pltpu.VMEM((steps, requests, heads, value_width), f32),
        in_specs=[smem, smem, anywhere, anywhere, vmem, anywhere, anywhere, anywhere],
        out_specs=vmem,
        scratch_shapes=[
            pltpu.VMEM(query_heads.shape, bf16),
            pltpu.VMEM(new_latent.shape, bf16),
            pltpu.VMEM((heads, nope, width), bf16),
            pltpu.VMEM((2, width, value_width), bf16),
            pltpu.VMEM((requests, packed, cached), bf16),
            pltpu.VMEM((requests, 4, rows, packed), bf16),
            pltpu.VMEM((tile, packed), bf16),
            pltpu.VMEM((2, 4 * rows, cached), f32),
            pltpu.VMEM((4 * rows, cached), bf16),
            pltpu.VMEM((requests, 4, rows, packed), bf16),
            pltpu.VMEM((requests, 2, rows, packed), bf16),
            pltpu.VMEM((requests, rows, packed), bf16),
            pltpu.VMEM((requests, rows, packed), f32),
            pltpu.VMEM((requests, rows, packed), bf16),
            pltpu.VMEM((requests, owners, 2 * rows // owners, width // 2 + tile), bf16),
            pltpu.VMEM((requests, seq_size, 2 * rows // owners, width // 2 + tile), bf16),
            pltpu.VMEM((requests, rows // owners, width), f32),
            pltpu.VMEM((owners, requests * rows // owners, value_width), bf16),
            dma((2,)),
            dma((requests,)),
            dma,
            dma,
        ]
        + [dma((requests,))] * 6
        + [dma((requests, 2))] * 2
        + [dma((requests,))] * 2
        + [dma((requests, owners)), dma((requests, seq_size)), dma((seq_size,)), dma((owners,))],
        compiler_params=pltpu.CompilerParams(
            collective_id=0, has_side_effects=True, vmem_limit_bytes=56 * 1024 * 1024
        ),
        cost_estimate=pl.CostEstimate(
            flops=2 * requests * 4 * rows * cached * (key_width + width),
            bytes_accessed=2 * requests * cached * key_width,
            transcendentals=requests * 4 * rows * cached,
        ),
    )(
        context_lengths,
        positions,
        query_heads,
        new_latent,
        jnp.asarray(frequencies(query_width - nope)),
        up_keys,
        up_values,
        jnp.swapaxes(latent_cache, 1, 2),
    )
    return attended.astype(bf16)


def solution(mesh):
    in_specs = (
        P(None, None, "head", None),
        P("head", None, None),
        P("head", None, None),
        P(None, ("seq", "head"), None),
        P(),
        P(),
        P(),
    )
    out_specs = P(None, None, "head", None)
    return jax.shard_map(
        functools.partial(on_device, mesh.shape["seq"]),
        mesh=mesh,
        in_specs=in_specs,
        out_specs=out_specs,
        check_vma=False,
    )
```

```python
import functools

import jax
import jax.numpy as jnp
import numpy as np
from jax import lax
from jax.experimental import pallas as pl
from jax.experimental.pallas import tpu as pltpu
from jax.sharding import PartitionSpec as P

MESH = pl.DeviceIdType.MESH
rope_base = 50000.0
masked_score = -1e30
lowest_peak = -1e29
log2_e = 1.4426950408889634
owners = 8
tile = 128
chunk = 512
turn_high = np.float32(6.28125)
turn_middle = np.float32(254 / 128 / 1024)
turn_low = np.float32(2 * np.pi - 6.28125 - 254 / 128 / 1024)


def iota(shape, axis):
    return lax.broadcasted_iota(jnp.int32, shape, axis)


def frequencies(rope_width):
    halfway = rope_width // 2
    inverse = np.power(rope_base, -2.0 * np.arange(halfway) / rope_width).astype(np.float32)
    return np.concatenate([inverse, inverse])[None, :]


def cos_sin(angles):
    turns = jnp.floor(angles * np.float32(0.5 / np.pi) + 0.5)
    rest = ((angles - turns * turn_high) - turns * turn_middle) - turns * turn_low
    return jnp.cos(rest), jnp.sin(rest)


def pack(values, peak, total):
    def term(v):
        return v.astype(jnp.bfloat16).astype(jnp.float32)

    p0 = term(peak)
    p1 = term(peak - p0)
    p2 = peak - p0 - p1
    t0 = term(total)
    t1 = total - t0
    shape = peak.shape[:-1] + (tile,)
    lane = iota(shape, len(shape) - 1)
    stats = jnp.where(lane == 0, p0, jnp.where(lane == 1, p1, jnp.where(lane == 2, p2, jnp.where(lane == 3, t0, t1))))
    return values.astype(jnp.bfloat16), stats.astype(jnp.bfloat16)


def unpack(packed, width):
    values = packed[..., :width].astype(jnp.float32)
    stats = packed[..., width:].astype(jnp.float32)
    peak = stats[..., 0:1] + stats[..., 1:2] + stats[..., 2:3]
    total = stats[..., 3:4] + stats[..., 4:5]
    return values, peak, total


def merge(one, two):
    (va, pa, ta), (vb, pb, tb) = one, two
    peak = jnp.maximum(pa, pb)
    wa, wb = jnp.exp2(pa - peak), jnp.exp2(pb - peak)
    return va * wa + vb * wb, peak, ta * wa + tb * wb


def kernel(
    seq_size,
    lengths,
    positions,
    q_hbm,
    new_hbm,
    frequency_ref,
    up_keys_hbm,
    up_values_hbm,
    cache_hbm,
    out_ref,
    q_ref,
    new_ref,
    up_keys,
    up_values,
    cache,
    queries,
    new_keys,
    scores,
    weights,
    partial,
    a_in,
    b_out,
    kept,
    b_in,
    c_out,
    c_in,
    mixed_latent,
    gathered,
    small_sem,
    load_sem,
    key_sem,
    value_sem,
    q1_send,
    q1_recv,
    qy_send,
    qy_recv,
    qf_send,
    qf_recv,
    a_send,
    a_recv,
    b_send,
    b_recv,
    c_send,
    c_recv,
    g_send,
    g_recv,
):
    steps, requests, heads, query_width = q_ref.shape
    nope, width = up_keys.shape[1], up_keys.shape[2]
    rope = query_width - nope
    rows_cached = cache.shape[2]
    rows = steps * heads
    piece = rows // owners
    half = width // 2
    all_rows = 4 * rows
    seq = lax.axis_index("seq")
    head = lax.axis_index("head")
    low = lax.rem(head, 2)
    high = lax.div(head, 2)
    near = head + 1 - 2 * low
    across = lax.rem(head + 2, 4)
    slot = seq * 4 + head
    owned = lax.rem(seq, owners)

    def at_head(h):
        return (seq, h)

    barrier = pltpu.get_barrier_semaphore()
    for h in (near, across):
        pl.semaphore_signal(barrier, inc=1, device_id=at_head(h), device_id_type=MESH)
    for d in range(1, seq_size):
        pl.semaphore_signal(barrier, inc=1, device_id=(lax.rem(seq + d, seq_size), head), device_id_type=MESH)

    key_load = pltpu.make_async_copy(up_keys_hbm, up_keys, key_sem)
    q_load = pltpu.make_async_copy(q_hbm, q_ref, small_sem.at[0])
    new_load = pltpu.make_async_copy(new_hbm, new_ref, small_sem.at[1])
    q_load.start()
    new_load.start()
    key_load.start()
    value_load = pltpu.make_async_copy(up_values_hbm.at[pl.ds(owned * 2, 2)], up_values, value_sem)

    def load(b):
        return pltpu.make_async_copy(cache_hbm.at[b], cache.at[b, pl.ds(0, width + rope)], load_sem.at[b])

    swap = (iota((rope, rope), 0) == lax.rem(iota((rope, rope), 1) + rope // 2, rope)).astype(jnp.bfloat16)
    grid_row = iota((steps * requests, rope), 0)
    grid = lax.div(grid_row, requests)
    for b in range(requests):
        grid = grid + jnp.where(lax.rem(grid_row, requests) == b, positions[b], 0)
    cosine, sine = cos_sin(grid.astype(jnp.float32) * frequency_ref[...])
    sine = jnp.where(iota((steps * requests, rope), 1) < rope // 2, -sine, sine)
    q_load.wait()
    flat = q_ref[...].reshape(steps * requests * heads, query_width)
    q_rope = flat[:, nope:]
    swapped = jnp.dot(q_rope, swap, preferred_element_type=jnp.float32)
    three = (steps * requests, heads, rope)
    rotated = (
        q_rope.astype(jnp.float32).reshape(three) * cosine[:, None, :] + swapped.reshape(three) * sine[:, None, :]
    )
    rotated = rotated.astype(jnp.bfloat16).reshape(steps * requests * heads, rope)
    rotated = jnp.concatenate([rotated, jnp.zeros_like(rotated)], axis=1)
    count = steps * requests * heads
    row = iota((count, count), 0)
    wanted = (row & (steps - 1)) * (requests * heads) + lax.div(row, rows) * heads + lax.div(lax.rem(row, rows), steps)
    order = (iota((count, count), 1) == wanted).astype(jnp.bfloat16)
    q_nope = jnp.dot(order, flat[:, :nope], preferred_element_type=jnp.float32).astype(jnp.bfloat16)
    rotated = jnp.dot(order, rotated, preferred_element_type=jnp.float32).astype(jnp.bfloat16)

    new_load.wait()
    new_flat = new_ref[...].astype(jnp.float32).reshape(steps * requests, width + rope).astype(jnp.bfloat16)
    new_rope = new_flat[:, width:]
    new_swapped = jnp.dot(new_rope, swap, preferred_element_type=jnp.float32)
    new_rotated = new_rope.astype(jnp.float32) * cosine + new_swapped * sine
    new_keys[...] = jnp.zeros_like(new_keys)
    new_keys[: steps * requests, :width] = new_flat[:, :width]
    new_keys[: steps * requests, width : width + rope] = new_rotated.astype(jnp.bfloat16)

    own_head = lax.div(lax.rem(iota((count, nope), 0), rows), steps)
    spread = jnp.concatenate(
        [jnp.where(own_head == h, q_nope.astype(jnp.float32), 0.0).astype(jnp.bfloat16) for h in range(heads)], axis=1
    )
    key_load.wait()
    for b in range(requests):
        load(b).start()
    value_load.start()
    latent = jnp.dot(spread, up_keys[...].reshape(heads * nope, width), preferred_element_type=jnp.float32)
    latent = latent.astype(jnp.bfloat16)
    for b in range(requests):
        queries[b, head, :, :width] = latent[b * rows : (b + 1) * rows]
        queries[b, head, :, width : width + tile] = rotated[b * rows : (b + 1) * rows]
        cache[b, width + rope :, :] = jnp.zeros((tile - rope, rows_cached), jnp.bfloat16)

    def remote(source, target, send, recv, device):
        return pltpu.make_async_remote_copy(
            src_ref=source, dst_ref=target, send_sem=send, recv_sem=recv, device_id=device, device_id_type=MESH
        )

    def q_near(b):
        block = queries.at[b, head]
        return remote(block, block, q1_send.at[b], q1_recv.at[b], at_head(near))

    def q_across(b):
        block = queries.at[b, head]
        return remote(block, block, qy_send.at[b], qy_recv.at[b], at_head(across))

    def q_forward(b):
        block = queries.at[b, across]
        return remote(block, block, qf_send.at[b], qf_recv.at[b], at_head(near))

    def a_copy(b, j):
        return remote(
            partial.at[b, 1 - low + 2 * j], a_in.at[b, j], a_send.at[b, j], a_recv.at[b, j], at_head(near)
        )

    def b_copy(b):
        return remote(b_out.at[b], b_in.at[b], b_send.at[b], b_recv.at[b], at_head(across))

    def c_copy(p, target, source):
        return remote(
            c_out.at[p, target], c_in.at[p, source], c_send.at[p, target], c_recv.at[p, source], (target, head)
        )

    def g_copy(d):
        target = lax.rem(seq + d, seq_size)
        return remote(
            gathered.at[owned], gathered.at[owned], g_send.at[target], g_recv.at[owned], (target, head)
        )

    pl.semaphore_wait(barrier, 2 + seq_size - 1)
    q_across(0).start()
    for b in range(requests):
        q_near(b).start()

    factor = log2_e * float(query_width) ** (-0.5)
    nt = (((1,), (1,)), ((), ()))
    spans = [slice(c * chunk, (c + 1) * chunk) for c in range(rows_cached // chunk)]

    def tiles(x, op, start):
        for i in range(x.shape[1] // tile):
            start = op(start, x[:, i * tile : (i + 1) * tile])
        return start

    def forward(b):
        q_across(b).wait_recv()
        if b + 1 < requests:
            q_across(b + 1).start()
        q_forward(b).start()

    def ready(b):
        q_near(b).wait_recv()
        q_forward(b).wait_recv()
        load(b).wait()

    def score(b, span, peaks):
        q = queries[b].reshape(all_rows, width + tile)
        s = jnp.dot(q, cache[b, :, span], preferred_element_type=jnp.float32)
        number = slot * rows_cached + span.start + iota((1, chunk), 1)
        x = s * factor + jnp.where(number < lengths[b], 0.0, masked_score)
        scores[b % 2, :, span] = x
        return tiles(x, jnp.maximum, peaks)

    def score_new(b, peaks):
        q = queries[b].reshape(all_rows, width + tile)
        s = lax.dot_general(q, new_keys[...], nt, preferred_element_type=jnp.float32)
        column = iota((all_rows, tile), 1)
        step = iota((all_rows, tile), 0) & (steps - 1)
        fresh = (
            (lax.rem(column, requests) == b)
            & (lax.div(column, requests) <= step)
            & (column < steps * requests)
            & (slot == 0)
        )
        x = s * factor + jnp.where(fresh, 0.0, masked_score)
        return x, jnp.max(jnp.maximum(peaks, x), axis=1, keepdims=True)

    lowest = jnp.full((all_rows, tile), lowest_peak, jnp.float32)

    def attend(b, x_new, peak):
        more = b + 1 < requests
        peaks = lowest
        fresh = jnp.exp2(x_new - peak)
        totals = fresh
        for span in spans:
            if more:
                peaks = score(b + 1, span, peaks)
            w = jnp.exp2(scores[b % 2, :, span] - peak)
            totals = tiles(w, jnp.add, totals)
            weights[:, span] = w.astype(jnp.bfloat16)
        if b + 2 < requests:
            forward(b + 2)
        if b >= 1:
            merge_near(b - 1)
        if b >= 2:
            merge_across(b - 2)
        if b >= 3:
            finish(b - 3)
        following = score_new(b + 1, peaks) if more else None
        mixed = jnp.dot(fresh.astype(jnp.bfloat16), new_keys[:, :width], preferred_element_type=jnp.float32)
        mixed += lax.dot_general(weights[...], cache[b, :width, :], nt, preferred_element_type=jnp.float32)
        values, stats = pack(mixed, peak, jnp.sum(totals, axis=1, keepdims=True))
        partial[b, :, :, :width] = values.reshape(4, rows, width)
        partial[b, :, :, width:] = stats.reshape(4, rows, tile)
        for j in range(2):
            a_copy(b, j).start()
        return following

    def merge_near(b):
        for j in range(2):
            a_copy(b, j).wait_recv()
        other = 1 - high
        merged = merge(
            unpack(partial[b, low + 2 * other], width),
            unpack(a_in[b, other], width),
        )
        values, stats = pack(*merged)
        b_out[b, :, :width] = values
        b_out[b, :, width:] = stats
        b_copy(b).start()
        values, peak, total = merge(
            unpack(partial[b, head], width),
            unpack(a_in[b, high], width),
        )
        kept[b, :, :width] = values
        kept[b, :, width:] = jnp.where(iota((rows, tile), 1) == 0, peak, total)

    def merge_across(b):
        b_copy(b).wait_recv()
        mine = (kept[b, :, :width], kept[b, :, width : width + 1], kept[b, :, width + 1 : width + 2])
        values, stats = pack(*merge(mine, unpack(b_in[b], width)))
        values = values.astype(jnp.float32).reshape(owners, piece, width)
        stats = stats.astype(jnp.float32).reshape(owners, piece, tile)
        c_out[b, :, :, :half] = jnp.concatenate([values[..., :half], values[..., half:]], axis=1).astype(jnp.bfloat16)
        c_out[b, :, :, half:] = jnp.concatenate([stats, stats], axis=1).astype(jnp.bfloat16)
        for d in range(0 if seq_size > owners else 1, owners):
            target = lax.rem(seq + d, owners)
            if d == 0:
                @pl.when(seq >= owners)
                def _():
                    c_copy(b, target, seq).start()
            else:
                c_copy(b, target, seq).start()

    def when_owner(fn):
        if seq_size > owners:
            pl.when(seq < owners)(fn)
        else:
            fn()

    def finish(b):
        def combine():
            c_in[b, owned] = c_out[b, owned]
            for d in range(1, seq_size):
                c_copy(b, owned, lax.rem(seq + d, seq_size)).wait_recv()
            values, peaks, totals = unpack(c_in[b], half)
            peak = jnp.max(peaks, axis=0, keepdims=True)
            scale = jnp.exp2(peaks - peak)
            mixed = jnp.sum(values * scale, axis=0) / jnp.sum(totals * scale, axis=0)
            mixed_latent[b, :, :half] = mixed[:piece]
            mixed_latent[b, :, half:] = mixed[piece:]

        when_owner(combine)

    def project():
        mixed = mixed_latent[...].reshape(requests * piece, width)
        second = lax.rem(iota(mixed.shape, 0), piece) >= steps
        wide = jnp.concatenate([jnp.where(second, 0.0, mixed), jnp.where(second, mixed, 0.0)], axis=1)
        w0 = wide.astype(jnp.bfloat16)
        rest = wide - w0.astype(jnp.float32)
        w1 = rest.astype(jnp.bfloat16)
        w2 = (rest - w1.astype(jnp.float32)).astype(jnp.bfloat16)
        matrix = up_values[...].reshape(2 * width, up_values.shape[2])
        result = sum(jnp.dot(w, matrix, preferred_element_type=jnp.float32) for w in (w2, w1, w0))
        gathered[owned] = result.astype(jnp.bfloat16)

    forward(0)
    ready(0)
    peaks = lowest
    for span in spans:
        peaks = score(0, span, peaks)
    following = score_new(0, peaks)
    forward(1)
    for b in range(requests):
        if b + 1 < requests:
            ready(b + 1)
        following = attend(b, *following)
    merge_near(requests - 1)
    merge_across(requests - 2)
    finish(requests - 3)
    value_load.wait()
    merge_across(requests - 1)
    finish(requests - 2)
    finish(requests - 1)

    def last():
        project()
        for d in range(1, seq_size):
            g_copy(d).start()

    when_owner(last)

    def from_owner(j):
        block = gathered.at[j]
        return remote(block, block, g_send.at[j], g_recv.at[j], (seq, near))

    for d in range(0 if seq_size > owners else 1, owners):
        source = lax.rem(seq + d, owners)
        if d == 0:
            @pl.when(seq >= owners)
            def _():
                from_owner(source).wait_recv()
        else:
            from_owner(source).wait_recv()

    per = rows * requests // owners
    row = iota((count, count), 0)
    s_of = lax.div(row, requests * heads)
    b_of = lax.rem(lax.div(row, heads), requests)
    h_of = lax.rem(row, heads)
    source = lax.div(h_of, 2) * per + b_of * piece + (h_of & 1) * steps + s_of
    back = (iota((count, count), 1) == source).astype(jnp.bfloat16)
    result = jnp.dot(back, gathered[...].reshape(count, -1), preferred_element_type=jnp.float32)
    out_ref[...] = result.reshape(out_ref.shape)

    for b in range(requests):
        q_near(b).wait_send()
        q_across(b).wait_send()
        q_forward(b).wait_send()
        for j in range(2):
            a_copy(b, j).wait_send()
        b_copy(b).wait_send()
    for p in range(requests):
        for d in range(0 if seq_size > owners else 1, owners):
            target = lax.rem(seq + d, owners)
            if d == 0:
                @pl.when(seq >= owners)
                def _():
                    c_copy(p, target, seq).wait_send()
            else:
                c_copy(p, target, seq).wait_send()

    def sent():
        for d in range(1, seq_size):
            g_copy(d).wait_send()

    when_owner(sent)


def on_device(seq_size, query_heads, up_keys, up_values, latent_cache, new_latent, context_lengths, positions):
    steps, requests, heads, query_width = query_heads.shape
    nope, width = up_keys.shape[1:]
    value_width = up_values.shape[2]
    key_width = latent_cache.shape[2]
    cached = latent_cache.shape[1]
    rows = steps * heads
    bf16, f32 = jnp.bfloat16, jnp.float32
    packed = width + tile
    dma = pltpu.SemaphoreType.DMA
    smem = pl.BlockSpec(memory_space=pltpu.SMEM)
    vmem = pl.BlockSpec(memory_space=pltpu.VMEM)
    anywhere = pl.BlockSpec(memory_space=pl.ANY)
    attended = pl.pallas_call(
        functools.partial(kernel, seq_size),
        out_shape=pltpu.VMEM((steps, requests, heads, value_width), f32),
        in_specs=[smem, smem, anywhere, anywhere, vmem, anywhere, anywhere, anywhere],
        out_specs=vmem,
        scratch_shapes=[
            pltpu.VMEM(query_heads.shape, bf16),
            pltpu.VMEM(new_latent.shape, bf16),
            pltpu.VMEM((heads, nope, width), bf16),
            pltpu.VMEM((2, width, value_width), bf16),
            pltpu.VMEM((requests, packed, cached), bf16),
            pltpu.VMEM((requests, 4, rows, packed), bf16),
            pltpu.VMEM((tile, packed), bf16),
            pltpu.VMEM((2, 4 * rows, cached), f32),
            pltpu.VMEM((4 * rows, cached), bf16),
            pltpu.VMEM((requests, 4, rows, packed), bf16),
            pltpu.VMEM((requests, 2, rows, packed), bf16),
            pltpu.VMEM((requests, rows, packed), bf16),
            pltpu.VMEM((requests, rows, packed), f32),
            pltpu.VMEM((requests, rows, packed), bf16),
            pltpu.VMEM((requests, owners, 2 * rows // owners, width // 2 + tile), bf16),
            pltpu.VMEM((requests, seq_size, 2 * rows // owners, width // 2 + tile), bf16),
            pltpu.VMEM((requests, rows // owners, width), f32),
            pltpu.VMEM((owners, requests * rows // owners, value_width), bf16),
            dma((2,)),
            dma((requests,)),
            dma,
            dma,
        ]
        + [dma((requests,))] * 6
        + [dma((requests, 2))] * 2
        + [dma((requests,))] * 2
        + [dma((requests, owners)), dma((requests, seq_size)), dma((seq_size,)), dma((owners,))],
        compiler_params=pltpu.CompilerParams(
            collective_id=0, has_side_effects=True, vmem_limit_bytes=56 * 1024 * 1024
        ),
        cost_estimate=pl.CostEstimate(
            flops=2 * requests * 4 * rows * cached * (key_width + width),
            bytes_accessed=2 * requests * cached * key_width,
            transcendentals=requests * 4 * rows * cached,
        ),
    )(
        context_lengths,
        positions,
        query_heads,
        new_latent,
        jnp.asarray(frequencies(query_width - nope)),
        up_keys,
        up_values,
        jnp.swapaxes(latent_cache, 1, 2),
    )
    return attended.astype(bf16)


def solution(mesh):
    in_specs = (
        P(None, None, "head", None),
        P("head", None, None),
        P("head", None, None),
        P(None, ("seq", "head"), None),
        P(),
        P(),
        P(),
    )
    out_specs = P(None, None, "head", None)
    return jax.shard_map(
        functools.partial(on_device, mesh.shape["seq"]),
        mesh=mesh,
        in_specs=in_specs,
        out_specs=out_specs,
        check_vma=False,
    )
```

```python
import functools

import jax
import jax.numpy as jnp
import numpy as np
from jax import lax
from jax.experimental import pallas as pl
from jax.experimental.pallas import tpu as pltpu
from jax.sharding import PartitionSpec as P

MESH = pl.DeviceIdType.MESH
rope_base = 50000.0
masked_score = -1e30
lowest_peak = -1e29
log2_e = 1.4426950408889634
owners = 8
tile = 128
chunk = 512
turn_high = np.float32(6.28125)
turn_middle = np.float32(254 / 128 / 1024)
turn_low = np.float32(2 * np.pi - 6.28125 - 254 / 128 / 1024)


def iota(shape, axis):
    return lax.broadcasted_iota(jnp.int32, shape, axis)


def frequencies(rope_width):
    halfway = rope_width // 2
    inverse = np.power(rope_base, -2.0 * np.arange(halfway) / rope_width).astype(np.float32)
    return np.concatenate([inverse, inverse])[None, :]


def cos_sin(angles):
    turns = jnp.floor(angles * np.float32(0.5 / np.pi) + 0.5)
    rest = ((angles - turns * turn_high) - turns * turn_middle) - turns * turn_low
    return jnp.cos(rest), jnp.sin(rest)


def pack(values, peak, total):
    def term(v):
        return v.astype(jnp.bfloat16).astype(jnp.float32)

    p0 = term(peak)
    p1 = term(peak - p0)
    p2 = peak - p0 - p1
    t0 = term(total)
    t1 = total - t0
    shape = peak.shape[:-1] + (tile,)
    lane = iota(shape, len(shape) - 1)
    stats = jnp.where(lane == 0, p0, jnp.where(lane == 1, p1, jnp.where(lane == 2, p2, jnp.where(lane == 3, t0, t1))))
    return values.astype(jnp.bfloat16), stats.astype(jnp.bfloat16)


def unpack(packed, width):
    values = packed[..., :width].astype(jnp.float32)
    stats = packed[..., width:].astype(jnp.float32)
    peak = stats[..., 0:1] + stats[..., 1:2] + stats[..., 2:3]
    total = stats[..., 3:4] + stats[..., 4:5]
    return values, peak, total


def merge(one, two):
    (va, pa, ta), (vb, pb, tb) = one, two
    peak = jnp.maximum(pa, pb)
    wa, wb = jnp.exp2(pa - peak), jnp.exp2(pb - peak)
    return va * wa + vb * wb, peak, ta * wa + tb * wb


def kernel(
    seq_size,
    lengths,
    positions,
    q_hbm,
    new_hbm,
    frequency_ref,
    up_keys_hbm,
    up_values_hbm,
    cache_hbm,
    out_ref,
    q_ref,
    new_ref,
    up_keys,
    up_values,
    cache,
    queries,
    new_keys,
    scores,
    weights,
    partial,
    a_in,
    b_out,
    kept,
    b_in,
    c_out,
    c_in,
    mixed_latent,
    gathered,
    small_sem,
    load_sem,
    key_sem,
    value_sem,
    q1_send,
    q1_recv,
    qy_send,
    qy_recv,
    qf_send,
    qf_recv,
    qx_send,
    qx_recv,
    a_send,
    a_recv,
    b_send,
    b_recv,
    c_send,
    c_recv,
    g_send,
    g_recv,
):
    steps, requests, heads, query_width = q_ref.shape
    nope, width = up_keys.shape[1], up_keys.shape[2]
    rope = query_width - nope
    rows_cached = cache.shape[2]
    rows = steps * heads
    piece = rows // owners
    half = width // 2
    all_rows = 4 * rows
    seq = lax.axis_index("seq")
    head = lax.axis_index("head")
    low = lax.rem(head, 2)
    high = lax.div(head, 2)
    near = head + 1 - 2 * low
    across = lax.rem(head + 2, 4)
    slot = seq * 4 + head
    side = lax.rem(seq, 2)
    owned = lax.rem(seq, owners)

    def at_head(h):
        return (seq, h)

    barrier = pltpu.get_barrier_semaphore()
    for h in (near, across):
        pl.semaphore_signal(barrier, inc=1, device_id=at_head(h), device_id_type=MESH)
    for d in range(1, seq_size):
        pl.semaphore_signal(barrier, inc=1, device_id=(lax.rem(seq + d, seq_size), head), device_id_type=MESH)

    key_load = pltpu.make_async_copy(up_keys_hbm, up_keys, key_sem)
    q_load = pltpu.make_async_copy(q_hbm, q_ref, small_sem.at[0])
    new_load = pltpu.make_async_copy(new_hbm, new_ref, small_sem.at[1])
    q_load.start()
    new_load.start()
    key_load.start()
    value_load = pltpu.make_async_copy(up_values_hbm.at[pl.ds(owned * 2, 2)], up_values, value_sem)

    def load(b):
        return pltpu.make_async_copy(cache_hbm.at[b], cache.at[b, pl.ds(0, width + rope)], load_sem.at[b])

    swap = (iota((rope, rope), 0) == lax.rem(iota((rope, rope), 1) + rope // 2, rope)).astype(jnp.bfloat16)
    grid_row = iota((steps * requests, rope), 0)
    grid = lax.div(grid_row, requests)
    for b in range(requests):
        grid = grid + jnp.where(lax.rem(grid_row, requests) == b, positions[b], 0)
    cosine, sine = cos_sin(grid.astype(jnp.float32) * frequency_ref[...])
    sine = jnp.where(iota((steps * requests, rope), 1) < rope // 2, -sine, sine)
    q_load.wait()
    flat = q_ref[...].reshape(steps * requests * heads, query_width)
    q_rope = flat[:, nope:]
    swapped = jnp.dot(q_rope, swap, preferred_element_type=jnp.float32)
    three = (steps * requests, heads, rope)
    rotated = (
        q_rope.astype(jnp.float32).reshape(three) * cosine[:, None, :] + swapped.reshape(three) * sine[:, None, :]
    )
    rotated = rotated.astype(jnp.bfloat16).reshape(steps * requests * heads, rope)
    rotated = jnp.concatenate([rotated, jnp.zeros_like(rotated)], axis=1)
    count = steps * requests * heads
    row = iota((count, count), 0)
    wanted = (row & (steps - 1)) * (requests * heads) + lax.div(row, rows) * heads + lax.div(lax.rem(row, rows), steps)
    order = (iota((count, count), 1) == wanted).astype(jnp.bfloat16)
    q_nope = jnp.dot(order, flat[:, :nope], preferred_element_type=jnp.float32).astype(jnp.bfloat16)
    rotated = jnp.dot(order, rotated, preferred_element_type=jnp.float32).astype(jnp.bfloat16)

    new_load.wait()
    new_flat = new_ref[...].astype(jnp.float32).reshape(steps * requests, width + rope).astype(jnp.bfloat16)
    new_rope = new_flat[:, width:]
    new_swapped = jnp.dot(new_rope, swap, preferred_element_type=jnp.float32)
    new_rotated = new_rope.astype(jnp.float32) * cosine + new_swapped * sine
    new_keys[...] = jnp.zeros_like(new_keys)
    new_keys[: steps * requests, :width] = new_flat[:, :width]
    new_keys[: steps * requests, width : width + rope] = new_rotated.astype(jnp.bfloat16)

    own_head = lax.div(lax.rem(iota((count, nope), 0), rows), steps)
    spread = jnp.concatenate(
        [jnp.where(own_head == h, q_nope.astype(jnp.float32), 0.0).astype(jnp.bfloat16) for h in range(heads)], axis=1
    )
    key_load.wait()
    for b in range(requests):
        load(b).start()
    value_load.start()
    latent = jnp.dot(spread, up_keys[...].reshape(heads * nope, width), preferred_element_type=jnp.float32)
    latent = latent.astype(jnp.bfloat16)
    for b in range(requests):
        queries[b, head, :, :width] = latent[b * rows : (b + 1) * rows]
        queries[b, head, :, width : width + tile] = rotated[b * rows : (b + 1) * rows]
        cache[b, width + rope :, :] = jnp.zeros((tile - rope, rows_cached), jnp.bfloat16)

    def remote(source, target, send, recv, device):
        return pltpu.make_async_remote_copy(
            src_ref=source, dst_ref=target, send_sem=send, recv_sem=recv, device_id=device, device_id_type=MESH
        )

    def q_near(b):
        block = queries.at[b, head]
        return remote(block, block, q1_send.at[b], q1_recv.at[b], at_head(near))

    def part_of(b, h, part):
        return queries.at[b, h, pl.ds(pl.multiple_of(part * (rows // 2), rows // 2), rows // 2)]

    def q_across(b):
        block = queries.at[b, head] if b == 0 else part_of(b, head, side)
        return remote(block, block, qy_send.at[b], qy_recv.at[b], at_head(across))

    def q_side(b):
        block = part_of(b, across, side)
        return remote(block, block, qx_send.at[b], qx_recv.at[b], (seq + 1 - 2 * side, head))

    def q_forward(b, last=False):
        if b == 0:
            block = queries.at[b, across]
        else:
            block = part_of(b, across, 1 - side if last else side)
        at = 2 * b + last
        return remote(block, block, qf_send.at[at], qf_recv.at[at], at_head(near))

    def a_copy(b, j):
        return remote(
            partial.at[b, 1 - low + 2 * j], a_in.at[b, j], a_send.at[b, j], a_recv.at[b, j], at_head(near)
        )

    def b_copy(b):
        return remote(b_out.at[b], b_in.at[b], b_send.at[b], b_recv.at[b], at_head(across))

    def c_copy(p, target, source):
        return remote(
            c_out.at[p, target], c_in.at[p, source], c_send.at[p, target], c_recv.at[p, source], (target, head)
        )

    def g_copy(d):
        target = lax.rem(seq + d, seq_size)
        return remote(
            gathered.at[owned], gathered.at[owned], g_send.at[target], g_recv.at[owned], (target, head)
        )

    pl.semaphore_wait(barrier, 2 + seq_size - 1)
    for b in range(requests):
        q_across(b).start()
    for b in range(requests):
        q_near(b).start()

    factor = log2_e * float(query_width) ** (-0.5)
    nt = (((1,), (1,)), ((), ()))
    spans = [slice(c * chunk, (c + 1) * chunk) for c in range(rows_cached // chunk)]

    def tiles(x, op, start):
        for i in range(x.shape[1] // tile):
            start = op(start, x[:, i * tile : (i + 1) * tile])
        return start

    def forward(b):
        q_across(b).wait_recv()
        if b > 0:
            q_side(b).start()
        q_forward(b).start()

    def forward_rest(b):
        q_side(b).wait_recv()
        q_forward(b, True).start()

    def ready(b):
        q_near(b).wait_recv()
        q_forward(b).wait_recv()
        if b > 0:
            q_forward(b, True).wait_recv()
        load(b).wait()

    def score(b, span, peaks):
        q = queries[b].reshape(all_rows, width + tile)
        s = jnp.dot(q, cache[b, :, span], preferred_element_type=jnp.float32)
        number = slot * rows_cached + span.start + iota((1, chunk), 1)
        x = s * factor + jnp.where(number < lengths[b], 0.0, masked_score)
        scores[b % 2, :, span] = x
        return tiles(x, jnp.maximum, peaks)

    def score_new(b, peaks):
        q = queries[b].reshape(all_rows, width + tile)
        s = lax.dot_general(q, new_keys[...], nt, preferred_element_type=jnp.float32)
        column = iota((all_rows, tile), 1)
        step = iota((all_rows, tile), 0) & (steps - 1)
        fresh = (
            (lax.rem(column, requests) == b)
            & (lax.div(column, requests) <= step)
            & (column < steps * requests)
            & (slot == 0)
        )
        x = s * factor + jnp.where(fresh, 0.0, masked_score)
        return x, jnp.max(jnp.maximum(peaks, x), axis=1, keepdims=True)

    lowest = jnp.full((all_rows, tile), lowest_peak, jnp.float32)

    def attend(b, x_new, peak):
        more = b + 1 < requests
        peaks = lowest
        fresh = jnp.exp2(x_new - peak)
        totals = fresh
        for span in spans:
            if more:
                peaks = score(b + 1, span, peaks)
            w = jnp.exp2(scores[b % 2, :, span] - peak)
            totals = tiles(w, jnp.add, totals)
            weights[:, span] = w.astype(jnp.bfloat16)
        if b == 0:
            for later in range(2, requests):
                forward_rest(later)
        if b >= 1:
            merge_near(b - 1)
        if b >= 2:
            merge_across(b - 2)
        if b >= 3:
            finish(b - 3)
        following = score_new(b + 1, peaks) if more else None
        mixed = jnp.dot(fresh.astype(jnp.bfloat16), new_keys[:, :width], preferred_element_type=jnp.float32)
        mixed += lax.dot_general(weights[...], cache[b, :width, :], nt, preferred_element_type=jnp.float32)
        values, stats = pack(mixed, peak, jnp.sum(totals, axis=1, keepdims=True))
        partial[b, :, :, :width] = values.reshape(4, rows, width)
        partial[b, :, :, width:] = stats.reshape(4, rows, tile)
        for j in range(2):
            a_copy(b, j).start()
        return following

    def merge_near(b):
        for j in range(2):
            a_copy(b, j).wait_recv()
        other = 1 - high
        merged = merge(
            unpack(partial[b, low + 2 * other], width),
            unpack(a_in[b, other], width),
        )
        values, stats = pack(*merged)
        b_out[b, :, :width] = values
        b_out[b, :, width:] = stats
        b_copy(b).start()
        values, peak, total = merge(
            unpack(partial[b, head], width),
            unpack(a_in[b, high], width),
        )
        kept[b, :, :width] = values
        kept[b, :, width:] = jnp.where(iota((rows, tile), 1) == 0, peak, total)

    def merge_across(b):
        b_copy(b).wait_recv()
        mine = (kept[b, :, :width], kept[b, :, width : width + 1], kept[b, :, width + 1 : width + 2])
        values, stats = pack(*merge(mine, unpack(b_in[b], width)))
        values = values.astype(jnp.float32).reshape(owners, piece, width)
        stats = stats.astype(jnp.float32).reshape(owners, piece, tile)
        c_out[b, :, :, :half] = jnp.concatenate([values[..., :half], values[..., half:]], axis=1).astype(jnp.bfloat16)
        c_out[b, :, :, half:] = jnp.concatenate([stats, stats], axis=1).astype(jnp.bfloat16)
        for d in range(0 if seq_size > owners else 1, owners):
            target = lax.rem(seq + d, owners)
            if d == 0:
                @pl.when(seq >= owners)
                def _():
                    c_copy(b, target, seq).start()
            else:
                c_copy(b, target, seq).start()

    def when_owner(fn):
        if seq_size > owners:
            pl.when(seq < owners)(fn)
        else:
            fn()

    def finish(b):
        def combine():
            c_in[b, owned] = c_out[b, owned]
            for d in range(1, seq_size):
                c_copy(b, owned, lax.rem(seq + d, seq_size)).wait_recv()
            values, peaks, totals = unpack(c_in[b], half)
            peak = jnp.max(peaks, axis=0, keepdims=True)
            scale = jnp.exp2(peaks - peak)
            mixed = jnp.sum(values * scale, axis=0) / jnp.sum(totals * scale, axis=0)
            mixed_latent[b, :, :half] = mixed[:piece]
            mixed_latent[b, :, half:] = mixed[piece:]

        when_owner(combine)

    def project():
        mixed = mixed_latent[...].reshape(requests * piece, width)
        second = lax.rem(iota(mixed.shape, 0), piece) >= steps
        wide = jnp.concatenate([jnp.where(second, 0.0, mixed), jnp.where(second, mixed, 0.0)], axis=1)
        w0 = wide.astype(jnp.bfloat16)
        rest = wide - w0.astype(jnp.float32)
        w1 = rest.astype(jnp.bfloat16)
        w2 = (rest - w1.astype(jnp.float32)).astype(jnp.bfloat16)
        matrix = up_values[...].reshape(2 * width, up_values.shape[2])
        result = sum(jnp.dot(w, matrix, preferred_element_type=jnp.float32) for w in (w2, w1, w0))
        gathered[owned] = result.astype(jnp.bfloat16)

    forward(0)
    forward(1)
    ready(0)
    peaks = lowest
    for span in spans:
        peaks = score(0, span, peaks)
    following = score_new(0, peaks)
    for b in range(2, requests):
        forward(b)
    forward_rest(1)
    for b in range(requests):
        if b + 1 < requests:
            ready(b + 1)
        following = attend(b, *following)
    merge_near(requests - 1)
    merge_across(requests - 2)
    finish(requests - 3)
    value_load.wait()
    merge_across(requests - 1)
    finish(requests - 2)
    finish(requests - 1)

    def last():
        project()
        for d in range(1, seq_size):
            g_copy(d).start()

    when_owner(last)

    def from_owner(j):
        block = gathered.at[j]
        return remote(block, block, g_send.at[j], g_recv.at[j], (seq, near))

    for d in range(0 if seq_size > owners else 1, owners):
        source = lax.rem(seq + d, owners)
        if d == 0:
            @pl.when(seq >= owners)
            def _():
                from_owner(source).wait_recv()
        else:
            from_owner(source).wait_recv()

    per = rows * requests // owners
    row = iota((count, count), 0)
    s_of = lax.div(row, requests * heads)
    b_of = lax.rem(lax.div(row, heads), requests)
    h_of = lax.rem(row, heads)
    source = lax.div(h_of, 2) * per + b_of * piece + (h_of & 1) * steps + s_of
    back = (iota((count, count), 1) == source).astype(jnp.bfloat16)
    result = jnp.dot(back, gathered[...].reshape(count, -1), preferred_element_type=jnp.float32)
    out_ref[...] = result.reshape(out_ref.shape)

    for b in range(requests):
        q_near(b).wait_send()
        q_across(b).wait_send()
        q_forward(b).wait_send()
        if b > 0:
            q_side(b).wait_send()
            q_forward(b, True).wait_send()
        for j in range(2):
            a_copy(b, j).wait_send()
        b_copy(b).wait_send()
    for p in range(requests):
        for d in range(0 if seq_size > owners else 1, owners):
            target = lax.rem(seq + d, owners)
            if d == 0:
                @pl.when(seq >= owners)
                def _():
                    c_copy(p, target, seq).wait_send()
            else:
                c_copy(p, target, seq).wait_send()

    def sent():
        for d in range(1, seq_size):
            g_copy(d).wait_send()

    when_owner(sent)


def on_device(seq_size, query_heads, up_keys, up_values, latent_cache, new_latent, context_lengths, positions):
    steps, requests, heads, query_width = query_heads.shape
    nope, width = up_keys.shape[1:]
    value_width = up_values.shape[2]
    key_width = latent_cache.shape[2]
    cached = latent_cache.shape[1]
    rows = steps * heads
    bf16, f32 = jnp.bfloat16, jnp.float32
    packed = width + tile
    dma = pltpu.SemaphoreType.DMA
    smem = pl.BlockSpec(memory_space=pltpu.SMEM)
    vmem = pl.BlockSpec(memory_space=pltpu.VMEM)
    anywhere = pl.BlockSpec(memory_space=pl.ANY)
    attended = pl.pallas_call(
        functools.partial(kernel, seq_size),
        out_shape=pltpu.VMEM((steps, requests, heads, value_width), f32),
        in_specs=[smem, smem, anywhere, anywhere, vmem, anywhere, anywhere, anywhere],
        out_specs=vmem,
        scratch_shapes=[
            pltpu.VMEM(query_heads.shape, bf16),
            pltpu.VMEM(new_latent.shape, bf16),
            pltpu.VMEM((heads, nope, width), bf16),
            pltpu.VMEM((2, width, value_width), bf16),
            pltpu.VMEM((requests, packed, cached), bf16),
            pltpu.VMEM((requests, 4, rows, packed), bf16),
            pltpu.VMEM((tile, packed), bf16),
            pltpu.VMEM((2, 4 * rows, cached), f32),
            pltpu.VMEM((4 * rows, cached), bf16),
            pltpu.VMEM((requests, 4, rows, packed), bf16),
            pltpu.VMEM((requests, 2, rows, packed), bf16),
            pltpu.VMEM((requests, rows, packed), bf16),
            pltpu.VMEM((requests, rows, packed), f32),
            pltpu.VMEM((requests, rows, packed), bf16),
            pltpu.VMEM((requests, owners, 2 * rows // owners, width // 2 + tile), bf16),
            pltpu.VMEM((requests, seq_size, 2 * rows // owners, width // 2 + tile), bf16),
            pltpu.VMEM((requests, rows // owners, width), f32),
            pltpu.VMEM((owners, requests * rows // owners, value_width), bf16),
            dma((2,)),
            dma((requests,)),
            dma,
            dma,
        ]
        + [dma((requests,))] * 4
        + [dma((2 * requests,))] * 2
        + [dma((requests,))] * 2
        + [dma((requests, 2))] * 2
        + [dma((requests,))] * 2
        + [dma((requests, owners)), dma((requests, seq_size)), dma((seq_size,)), dma((owners,))],
        compiler_params=pltpu.CompilerParams(
            collective_id=0, has_side_effects=True, vmem_limit_bytes=56 * 1024 * 1024
        ),
        cost_estimate=pl.CostEstimate(
            flops=2 * requests * 4 * rows * cached * (key_width + width),
            bytes_accessed=2 * requests * cached * key_width,
            transcendentals=requests * 4 * rows * cached,
        ),
    )(
        context_lengths,
        positions,
        query_heads,
        new_latent,
        jnp.asarray(frequencies(query_width - nope)),
        up_keys,
        up_values,
        jnp.swapaxes(latent_cache, 1, 2),
    )
    return attended.astype(bf16)


def solution(mesh):
    in_specs = (
        P(None, None, "head", None),
        P("head", None, None),
        P("head", None, None),
        P(None, ("seq", "head"), None),
        P(),
        P(),
        P(),
    )
    out_specs = P(None, None, "head", None)
    return jax.shard_map(
        functools.partial(on_device, mesh.shape["seq"]),
        mesh=mesh,
        in_specs=in_specs,
        out_specs=out_specs,
        check_vma=False,
    )
```

```python
import functools

import jax
import jax.numpy as jnp
import numpy as np
from jax import lax
from jax.experimental import pallas as pl
from jax.experimental.pallas import tpu as pltpu
from jax.sharding import PartitionSpec as P

MESH = pl.DeviceIdType.MESH
rope_base = 50000.0
masked_score = -1e30
lowest_peak = -1e29
log2_e = 1.4426950408889634
owners = 8
tile = 128
chunk = 512
turn_high = np.float32(6.28125)
turn_middle = np.float32(254 / 128 / 1024)
turn_low = np.float32(2 * np.pi - 6.28125 - 254 / 128 / 1024)


def iota(shape, axis):
    return lax.broadcasted_iota(jnp.int32, shape, axis)


def frequencies(rope_width):
    halfway = rope_width // 2
    inverse = np.power(rope_base, -2.0 * np.arange(halfway) / rope_width).astype(np.float32)
    return np.concatenate([inverse, inverse])[None, :]


def cos_sin(angles):
    turns = jnp.floor(angles * np.float32(0.5 / np.pi) + 0.5)
    rest = ((angles - turns * turn_high) - turns * turn_middle) - turns * turn_low
    return jnp.cos(rest), jnp.sin(rest)


def pack(values, peak, total):
    def term(v):
        return v.astype(jnp.bfloat16).astype(jnp.float32)

    p0 = term(peak)
    p1 = term(peak - p0)
    p2 = peak - p0 - p1
    t0 = term(total)
    t1 = total - t0
    shape = peak.shape[:-1] + (tile,)
    lane = iota(shape, len(shape) - 1)
    stats = jnp.where(lane == 0, p0, jnp.where(lane == 1, p1, jnp.where(lane == 2, p2, jnp.where(lane == 3, t0, t1))))
    return values.astype(jnp.bfloat16), stats.astype(jnp.bfloat16)


def unpack(packed, width, spread):
    values = packed[..., :width].astype(jnp.float32)
    stats = packed[..., width:]
    shape = stats.shape
    both = jnp.dot(stats.reshape(-1, tile), spread, preferred_element_type=jnp.float32)
    return values, both[:, :tile].reshape(shape), both[:, tile:].reshape(shape)


def by_tile(values, factor):
    parts = [values[..., i : i + tile] * factor for i in range(0, values.shape[-1], tile)]
    return jnp.concatenate(parts, axis=-1)


def merge(one, two):
    (va, pa, ta), (vb, pb, tb) = one, two
    peak = jnp.maximum(pa, pb)
    wa, wb = jnp.exp2(pa - peak), jnp.exp2(pb - peak)
    return by_tile(va, wa) + by_tile(vb, wb), peak, ta * wa + tb * wb


def kernel(
    seq_size,
    lengths,
    positions,
    q_hbm,
    new_hbm,
    frequency_ref,
    up_keys_hbm,
    up_values_hbm,
    cache_hbm,
    out_ref,
    q_ref,
    new_ref,
    up_keys,
    up_values,
    cache,
    queries,
    new_keys,
    scores,
    weights,
    partial,
    a_in,
    b_out,
    kept,
    b_in,
    c_out,
    c_in,
    mixed_latent,
    gathered,
    small_sem,
    load_sem,
    key_sem,
    value_sem,
    q1_send,
    q1_recv,
    qy_send,
    qy_recv,
    qf_send,
    qf_recv,
    qx_send,
    qx_recv,
    a_send,
    a_recv,
    b_send,
    b_recv,
    c_send,
    c_recv,
    g_send,
    g_recv,
):
    steps, requests, heads, query_width = q_ref.shape
    nope, width = up_keys.shape[1], up_keys.shape[2]
    rope = query_width - nope
    rows_cached = cache.shape[2]
    rows = steps * heads
    piece = rows // owners
    half = width // 2
    all_rows = 4 * rows
    seq = lax.axis_index("seq")
    head = lax.axis_index("head")
    low = lax.rem(head, 2)
    high = lax.div(head, 2)
    near = head + 1 - 2 * low
    across = lax.rem(head + 2, 4)
    slot = seq * 4 + head
    side = lax.rem(seq, 2)
    owned = lax.rem(seq, owners)

    def at_head(h):
        return (seq, h)

    barrier = pltpu.get_barrier_semaphore()
    for h in (near, across):
        pl.semaphore_signal(barrier, inc=1, device_id=at_head(h), device_id_type=MESH)
    for d in range(1, seq_size):
        pl.semaphore_signal(barrier, inc=1, device_id=(lax.rem(seq + d, seq_size), head), device_id_type=MESH)

    key_load = pltpu.make_async_copy(up_keys_hbm, up_keys, key_sem)
    q_load = pltpu.make_async_copy(q_hbm, q_ref, small_sem.at[0])
    new_load = pltpu.make_async_copy(new_hbm, new_ref, small_sem.at[1])
    q_load.start()
    new_load.start()
    key_load.start()
    value_load = pltpu.make_async_copy(up_values_hbm.at[pl.ds(owned * 2, 2)], up_values, value_sem)

    def load(b):
        return pltpu.make_async_copy(cache_hbm.at[b], cache.at[b, pl.ds(0, width + rope)], load_sem.at[b])

    swap = (iota((rope, rope), 0) == lax.rem(iota((rope, rope), 1) + rope // 2, rope)).astype(jnp.bfloat16)
    grid_row = iota((steps * requests, rope), 0)
    grid = lax.div(grid_row, requests)
    for b in range(requests):
        grid = grid + jnp.where(lax.rem(grid_row, requests) == b, positions[b], 0)
    cosine, sine = cos_sin(grid.astype(jnp.float32) * frequency_ref[...])
    sine = jnp.where(iota((steps * requests, rope), 1) < rope // 2, -sine, sine)
    q_load.wait()
    flat = q_ref[...].reshape(steps * requests * heads, query_width)
    q_rope = flat[:, nope:]
    swapped = jnp.dot(q_rope, swap, preferred_element_type=jnp.float32)
    three = (steps * requests, heads, rope)
    rotated = (
        q_rope.astype(jnp.float32).reshape(three) * cosine[:, None, :] + swapped.reshape(three) * sine[:, None, :]
    )
    rotated = rotated.astype(jnp.bfloat16).reshape(steps * requests * heads, rope)
    rotated = jnp.concatenate([rotated, jnp.zeros_like(rotated)], axis=1)
    count = steps * requests * heads
    row = iota((count, count), 0)
    wanted = (row & (steps - 1)) * (requests * heads) + lax.div(row, rows) * heads + lax.div(lax.rem(row, rows), steps)
    order = (iota((count, count), 1) == wanted).astype(jnp.bfloat16)
    q_nope = jnp.dot(order, flat[:, :nope], preferred_element_type=jnp.float32).astype(jnp.bfloat16)
    rotated = jnp.dot(order, rotated, preferred_element_type=jnp.float32).astype(jnp.bfloat16)

    new_load.wait()
    new_flat = new_ref[...].astype(jnp.float32).reshape(steps * requests, width + rope).astype(jnp.bfloat16)
    new_rope = new_flat[:, width:]
    new_swapped = jnp.dot(new_rope, swap, preferred_element_type=jnp.float32)
    new_rotated = new_rope.astype(jnp.float32) * cosine + new_swapped * sine
    new_keys[...] = jnp.zeros_like(new_keys)
    new_keys[: steps * requests, :width] = new_flat[:, :width]
    new_keys[: steps * requests, width : width + rope] = new_rotated.astype(jnp.bfloat16)

    own_head = lax.div(lax.rem(iota((count, nope), 0), rows), steps)
    spread = jnp.concatenate(
        [jnp.where(own_head == h, q_nope.astype(jnp.float32), 0.0).astype(jnp.bfloat16) for h in range(heads)], axis=1
    )
    key_load.wait()
    for b in range(requests):
        load(b).start()
    value_load.start()
    latent = jnp.dot(spread, up_keys[...].reshape(heads * nope, width), preferred_element_type=jnp.float32)
    latent = latent.astype(jnp.bfloat16)
    for b in range(requests):
        queries[b, head, :, :width] = latent[b * rows : (b + 1) * rows]
        queries[b, head, :, width : width + tile] = rotated[b * rows : (b + 1) * rows]
        cache[b, width + rope :, :] = jnp.zeros((tile - rope, rows_cached), jnp.bfloat16)

    def remote(source, target, send, recv, device):
        return pltpu.make_async_remote_copy(
            src_ref=source, dst_ref=target, send_sem=send, recv_sem=recv, device_id=device, device_id_type=MESH
        )

    def q_near(b):
        block = queries.at[b, head]
        return remote(block, block, q1_send.at[b], q1_recv.at[b], at_head(near))

    def part_of(b, h, part):
        return queries.at[b, h, pl.ds(pl.multiple_of(part * (rows // 2), rows // 2), rows // 2)]

    def q_across(b):
        block = queries.at[b, head] if b == 0 else part_of(b, head, side)
        return remote(block, block, qy_send.at[b], qy_recv.at[b], at_head(across))

    def q_side(b):
        block = part_of(b, across, side)
        return remote(block, block, qx_send.at[b], qx_recv.at[b], (seq + 1 - 2 * side, head))

    def q_forward(b, last=False):
        if b == 0:
            block = queries.at[b, across]
        else:
            block = part_of(b, across, 1 - side if last else side)
        at = 2 * b + last
        return remote(block, block, qf_send.at[at], qf_recv.at[at], at_head(near))

    def a_copy(b, j):
        return remote(
            partial.at[b, 1 - low + 2 * j], a_in.at[b, j], a_send.at[b, j], a_recv.at[b, j], at_head(near)
        )

    def b_copy(b):
        return remote(b_out.at[b], b_in.at[b], b_send.at[b], b_recv.at[b], at_head(across))

    def c_copy(p, target, source):
        return remote(
            c_out.at[p, target], c_in.at[p, source], c_send.at[p, target], c_recv.at[p, source], (target, head)
        )

    def g_copy(d):
        target = lax.rem(seq + d, seq_size)
        return remote(
            gathered.at[owned], gathered.at[owned], g_send.at[target], g_recv.at[owned], (target, head)
        )

    pl.semaphore_wait(barrier, 2 + seq_size - 1)
    for b in range(requests):
        q_across(b).start()
    for b in range(requests):
        q_near(b).start()

    term, to_total = iota((tile, 2 * tile), 0), iota((tile, 2 * tile), 1) >= tile
    terms = (~to_total & (term < 3)) | (to_total & (term >= 3) & (term < 5))
    ones_at = jnp.where(terms, 1.0, 0.0).astype(jnp.bfloat16)

    factor = log2_e * float(query_width) ** (-0.5)
    nt = (((1,), (1,)), ((), ()))
    spans = [slice(c * chunk, (c + 1) * chunk) for c in range(rows_cached // chunk)]

    def tiles(x, op, start):
        for i in range(x.shape[1] // tile):
            start = op(start, x[:, i * tile : (i + 1) * tile])
        return start

    def forward(b):
        q_across(b).wait_recv()
        if b > 0:
            q_side(b).start()
        q_forward(b).start()

    def forward_rest(b):
        q_side(b).wait_recv()
        q_forward(b, True).start()

    def ready(b):
        q_near(b).wait_recv()
        q_forward(b).wait_recv()
        if b > 0:
            q_forward(b, True).wait_recv()
        load(b).wait()

    def score(b, span, peaks):
        q = queries[b].reshape(all_rows, width + tile)
        s = jnp.dot(q, cache[b, :, span], preferred_element_type=jnp.float32)
        number = slot * rows_cached + span.start + iota((1, chunk), 1)
        x = s * factor + jnp.where(number < lengths[b], 0.0, masked_score)
        scores[b % 2, :, span] = x
        return tiles(x, jnp.maximum, peaks)

    def score_new(b, peaks):
        q = queries[b].reshape(all_rows, width + tile)
        s = lax.dot_general(q, new_keys[...], nt, preferred_element_type=jnp.float32)
        column = iota((all_rows, tile), 1)
        step = iota((all_rows, tile), 0) & (steps - 1)
        fresh = (
            (lax.rem(column, requests) == b)
            & (lax.div(column, requests) <= step)
            & (column < steps * requests)
            & (slot == 0)
        )
        x = s * factor + jnp.where(fresh, 0.0, masked_score)
        peak = jnp.max(jnp.maximum(peaks, x), axis=1, keepdims=True)
        return x, jnp.broadcast_to(peak, (all_rows, tile))

    lowest = jnp.full((all_rows, tile), lowest_peak, jnp.float32)

    def attend(b, x_new, peak):
        more = b + 1 < requests
        peaks = lowest
        fresh = jnp.exp2(x_new - peak)
        totals = fresh
        for span in spans:
            if more:
                peaks = score(b + 1, span, peaks)
            w = jnp.exp2(scores[b % 2, :, span] - jnp.concatenate([peak] * (chunk // tile), axis=1))
            totals = tiles(w, jnp.add, totals)
            weights[:, span] = w.astype(jnp.bfloat16)
        if b == 0:
            for later in range(2, requests):
                forward_rest(later)
        if b >= 1:
            merge_near(b - 1)
        following = score_new(b + 1, peaks) if more else None
        mixed = jnp.dot(fresh.astype(jnp.bfloat16), new_keys[:, :width], preferred_element_type=jnp.float32)
        mixed += lax.dot_general(weights[...], cache[b, :width, :], nt, preferred_element_type=jnp.float32)
        values, stats = pack(mixed, peak, jnp.broadcast_to(jnp.sum(totals, axis=1, keepdims=True), peak.shape))
        partial[b, :, :, :width] = values.reshape(4, rows, width)
        partial[b, :, :, width:] = stats.reshape(4, rows, tile)
        for j in range(2):
            a_copy(b, j).start()
        if b >= 2:
            merge_across(b - 2)
        if b >= 3:
            finish(b - 3)
        return following

    def merge_near(b):
        for j in range(2):
            a_copy(b, j).wait_recv()
        other = 1 - high
        merged = merge(
            unpack(partial[b, low + 2 * other], width, ones_at),
            unpack(a_in[b, other], width, ones_at),
        )
        values, stats = pack(*merged)
        b_out[b, :, :width] = values
        b_out[b, :, width:] = stats
        b_copy(b).start()
        values, peak, total = merge(
            unpack(partial[b, head], width, ones_at),
            unpack(a_in[b, high], width, ones_at),
        )
        kept[b, :, :width] = values
        kept[b, :, width : width + tile] = peak
        kept[b, :, width + tile :] = total

    def merge_across(b):
        b_copy(b).wait_recv()
        mine = (kept[b, :, :width], kept[b, :, width : width + tile], kept[b, :, width + tile :])
        values, stats = pack(*merge(mine, unpack(b_in[b], width, ones_at)))
        values = values.astype(jnp.float32).reshape(owners, piece, width)
        stats = stats.astype(jnp.float32).reshape(owners, piece, tile)
        c_out[b, :, :, :half] = jnp.concatenate([values[..., :half], values[..., half:]], axis=1).astype(jnp.bfloat16)
        c_out[b, :, :, half:] = jnp.concatenate([stats, stats], axis=1).astype(jnp.bfloat16)
        for d in range(0 if seq_size > owners else 1, owners):
            target = lax.rem(seq + d, owners)
            if d == 0:
                @pl.when(seq >= owners)
                def _():
                    c_copy(b, target, seq).start()
            else:
                c_copy(b, target, seq).start()

    def when_owner(fn):
        if seq_size > owners:
            pl.when(seq < owners)(fn)
        else:
            fn()

    def finish(b):
        def combine():
            c_in[b, owned] = c_out[b, owned]
            for d in range(1, seq_size):
                c_copy(b, owned, lax.rem(seq + d, seq_size)).wait_recv()
            values, peaks, totals = unpack(c_in[b], half, ones_at)
            peak = jnp.max(peaks, axis=0, keepdims=True)
            scale = jnp.exp2(peaks - peak)
            mixed = by_tile(jnp.sum(by_tile(values, scale), axis=0), 1.0 / jnp.sum(totals * scale, axis=0))
            mixed_latent[b, :, :half] = mixed[:piece]
            mixed_latent[b, :, half:] = mixed[piece:]

        when_owner(combine)

    def project():
        mixed = mixed_latent[...].reshape(requests * piece, width)
        second = lax.rem(iota(mixed.shape, 0), piece) >= steps
        wide = jnp.concatenate([jnp.where(second, 0.0, mixed), jnp.where(second, mixed, 0.0)], axis=1)
        w0 = wide.astype(jnp.bfloat16)
        rest = wide - w0.astype(jnp.float32)
        w1 = rest.astype(jnp.bfloat16)
        w2 = (rest - w1.astype(jnp.float32)).astype(jnp.bfloat16)
        matrix = up_values[...].reshape(2 * width, up_values.shape[2])
        result = sum(jnp.dot(w, matrix, preferred_element_type=jnp.float32) for w in (w2, w1, w0))
        gathered[owned] = result.astype(jnp.bfloat16)

    forward(0)
    forward(1)
    ready(0)
    peaks = lowest
    for span in spans:
        peaks = score(0, span, peaks)
    following = score_new(0, peaks)
    for b in range(2, requests):
        forward(b)
    forward_rest(1)
    for b in range(requests):
        if b + 1 < requests:
            ready(b + 1)
        following = attend(b, *following)
    merge_near(requests - 1)
    merge_across(requests - 2)
    finish(requests - 3)
    value_load.wait()
    merge_across(requests - 1)
    finish(requests - 2)
    finish(requests - 1)

    def last():
        project()
        for d in range(1, seq_size):
            g_copy(d).start()

    when_owner(last)

    def from_owner(j):
        block = gathered.at[j]
        return remote(block, block, g_send.at[j], g_recv.at[j], (seq, near))

    for d in range(0 if seq_size > owners else 1, owners):
        source = lax.rem(seq + d, owners)
        if d == 0:
            @pl.when(seq >= owners)
            def _():
                from_owner(source).wait_recv()
        else:
            from_owner(source).wait_recv()

    per = rows * requests // owners
    row = iota((count, count), 0)
    s_of = lax.div(row, requests * heads)
    b_of = lax.rem(lax.div(row, heads), requests)
    h_of = lax.rem(row, heads)
    source = lax.div(h_of, 2) * per + b_of * piece + (h_of & 1) * steps + s_of
    back = (iota((count, count), 1) == source).astype(jnp.bfloat16)
    result = jnp.dot(back, gathered[...].reshape(count, -1), preferred_element_type=jnp.float32)
    out_ref[...] = result.reshape(out_ref.shape)

    for b in range(requests):
        q_near(b).wait_send()
        q_across(b).wait_send()
        q_forward(b).wait_send()
        if b > 0:
            q_side(b).wait_send()
            q_forward(b, True).wait_send()
        for j in range(2):
            a_copy(b, j).wait_send()
        b_copy(b).wait_send()
    for p in range(requests):
        for d in range(0 if seq_size > owners else 1, owners):
            target = lax.rem(seq + d, owners)
            if d == 0:
                @pl.when(seq >= owners)
                def _():
                    c_copy(p, target, seq).wait_send()
            else:
                c_copy(p, target, seq).wait_send()

    def sent():
        for d in range(1, seq_size):
            g_copy(d).wait_send()

    when_owner(sent)


def on_device(seq_size, query_heads, up_keys, up_values, latent_cache, new_latent, context_lengths, positions):
    steps, requests, heads, query_width = query_heads.shape
    nope, width = up_keys.shape[1:]
    value_width = up_values.shape[2]
    key_width = latent_cache.shape[2]
    cached = latent_cache.shape[1]
    rows = steps * heads
    bf16, f32 = jnp.bfloat16, jnp.float32
    packed = width + tile
    dma = pltpu.SemaphoreType.DMA
    smem = pl.BlockSpec(memory_space=pltpu.SMEM)
    vmem = pl.BlockSpec(memory_space=pltpu.VMEM)
    anywhere = pl.BlockSpec(memory_space=pl.ANY)
    attended = pl.pallas_call(
        functools.partial(kernel, seq_size),
        out_shape=pltpu.VMEM((steps, requests, heads, value_width), f32),
        in_specs=[smem, smem, anywhere, anywhere, vmem, anywhere, anywhere, anywhere],
        out_specs=vmem,
        scratch_shapes=[
            pltpu.VMEM(query_heads.shape, bf16),
            pltpu.VMEM(new_latent.shape, bf16),
            pltpu.VMEM((heads, nope, width), bf16),
            pltpu.VMEM((2, width, value_width), bf16),
            pltpu.VMEM((requests, packed, cached), bf16),
            pltpu.VMEM((requests, 4, rows, packed), bf16),
            pltpu.VMEM((tile, packed), bf16),
            pltpu.VMEM((2, 4 * rows, cached), f32),
            pltpu.VMEM((4 * rows, cached), bf16),
            pltpu.VMEM((requests, 4, rows, packed), bf16),
            pltpu.VMEM((requests, 2, rows, packed), bf16),
            pltpu.VMEM((requests, rows, packed), bf16),
            pltpu.VMEM((requests, rows, packed + tile), f32),
            pltpu.VMEM((requests, rows, packed), bf16),
            pltpu.VMEM((requests, owners, 2 * rows // owners, width // 2 + tile), bf16),
            pltpu.VMEM((requests, seq_size, 2 * rows // owners, width // 2 + tile), bf16),
            pltpu.VMEM((requests, rows // owners, width), f32),
            pltpu.VMEM((owners, requests * rows // owners, value_width), bf16),
            dma((2,)),
            dma((requests,)),
            dma,
            dma,
        ]
        + [dma((requests,))] * 4
        + [dma((2 * requests,))] * 2
        + [dma((requests,))] * 2
        + [dma((requests, 2))] * 2
        + [dma((requests,))] * 2
        + [dma((requests, owners)), dma((requests, seq_size)), dma((seq_size,)), dma((owners,))],
        compiler_params=pltpu.CompilerParams(
            collective_id=0, has_side_effects=True, vmem_limit_bytes=56 * 1024 * 1024
        ),
        cost_estimate=pl.CostEstimate(
            flops=2 * requests * 4 * rows * cached * (key_width + width),
            bytes_accessed=2 * requests * cached * key_width,
            transcendentals=requests * 4 * rows * cached,
        ),
    )(
        context_lengths,
        positions,
        query_heads,
        new_latent,
        jnp.asarray(frequencies(query_width - nope)),
        up_keys,
        up_values,
        jnp.swapaxes(latent_cache, 1, 2),
    )
    return attended.astype(bf16)


def solution(mesh):
    in_specs = (
        P(None, None, "head", None),
        P("head", None, None),
        P("head", None, None),
        P(None, ("seq", "head"), None),
        P(),
        P(),
        P(),
    )
    out_specs = P(None, None, "head", None)
    return jax.shard_map(
        functools.partial(on_device, mesh.shape["seq"]),
        mesh=mesh,
        in_specs=in_specs,
        out_specs=out_specs,
        check_vma=False,
    )
```

```python
import functools

import jax
import jax.numpy as jnp
import numpy as np
from jax import lax
from jax.experimental import pallas as pl
from jax.experimental.pallas import tpu as pltpu
from jax.sharding import PartitionSpec as P

MESH = pl.DeviceIdType.MESH
rope_base = 50000.0
masked_score = -1e30
lowest_peak = -1e29
log2_e = 1.4426950408889634
owners = 8
tile = 128
chunk = 512
turn_high = np.float32(6.28125)
turn_middle = np.float32(254 / 128 / 1024)
turn_low = np.float32(2 * np.pi - 6.28125 - 254 / 128 / 1024)


def iota(shape, axis):
    return lax.broadcasted_iota(jnp.int32, shape, axis)


def frequencies(rope_width):
    halfway = rope_width // 2
    inverse = np.power(rope_base, -2.0 * np.arange(halfway) / rope_width).astype(np.float32)
    return np.concatenate([inverse, inverse])[None, :]


def cos_sin(angles):
    turns = jnp.floor(angles * np.float32(0.5 / np.pi) + 0.5)
    rest = ((angles - turns * turn_high) - turns * turn_middle) - turns * turn_low
    return jnp.cos(rest), jnp.sin(rest)


def pack(values, peak, total):
    def term(v):
        return v.astype(jnp.bfloat16).astype(jnp.float32)

    p0 = term(peak)
    p1 = term(peak - p0)
    p2 = peak - p0 - p1
    t0 = term(total)
    t1 = total - t0
    shape = peak.shape[:-1] + (tile,)
    lane = iota(shape, len(shape) - 1)
    stats = jnp.where(lane == 0, p0, jnp.where(lane == 1, p1, jnp.where(lane == 2, p2, jnp.where(lane == 3, t0, t1))))
    return values.astype(jnp.bfloat16), stats.astype(jnp.bfloat16)


def unpack(packed, width, spread):
    values = packed[..., :width].astype(jnp.float32)
    stats = packed[..., width:]
    shape = stats.shape
    both = jnp.dot(stats.reshape(-1, tile), spread, preferred_element_type=jnp.float32)
    return values, both[:, :tile].reshape(shape), both[:, tile:].reshape(shape)


def by_tile(values, factor):
    parts = [values[..., i : i + tile] * factor for i in range(0, values.shape[-1], tile)]
    return jnp.concatenate(parts, axis=-1)


def merge(one, two):
    (va, pa, ta), (vb, pb, tb) = one, two
    peak = jnp.maximum(pa, pb)
    wa, wb = jnp.exp2(pa - peak), jnp.exp2(pb - peak)
    return by_tile(va, wa) + by_tile(vb, wb), peak, ta * wa + tb * wb


def kernel(
    seq_size,
    lengths,
    positions,
    q_hbm,
    new_hbm,
    frequency_ref,
    up_keys_hbm,
    up_values_hbm,
    cache_hbm,
    out_ref,
    q_ref,
    new_ref,
    up_keys,
    up_values,
    cache,
    queries,
    new_keys,
    scores,
    weights,
    partial,
    a_in,
    b_out,
    kept,
    b_in,
    c_out,
    c_in,
    mixed_latent,
    gathered,
    small_sem,
    load_sem,
    key_sem,
    value_sem,
    q1_send,
    q1_recv,
    qy_send,
    qy_recv,
    qf_send,
    qf_recv,
    qx_send,
    qx_recv,
    a_send,
    a_recv,
    b_send,
    b_recv,
    c_send,
    c_recv,
    g_send,
    g_recv,
):
    steps, requests, heads, query_width = q_ref.shape
    nope, width = up_keys.shape[1], up_keys.shape[2]
    rope = query_width - nope
    rows_cached = cache.shape[2]
    rows = steps * heads
    piece = rows // owners
    half = width // 2
    all_rows = 4 * rows
    seq = lax.axis_index("seq")
    head = lax.axis_index("head")
    low = lax.rem(head, 2)
    high = lax.div(head, 2)
    near = head + 1 - 2 * low
    across = lax.rem(head + 2, 4)
    slot = seq * 4 + head
    side = lax.rem(seq, 2)
    owned = lax.rem(seq, owners)

    def at_head(h):
        return (seq, h)

    barrier = pltpu.get_barrier_semaphore()
    for h in (near, across):
        pl.semaphore_signal(barrier, inc=1, device_id=at_head(h), device_id_type=MESH)
    for d in range(1, seq_size):
        pl.semaphore_signal(barrier, inc=1, device_id=(lax.rem(seq + d, seq_size), head), device_id_type=MESH)

    key_load = pltpu.make_async_copy(up_keys_hbm, up_keys, key_sem)
    q_load = pltpu.make_async_copy(q_hbm, q_ref, small_sem.at[0])
    new_load = pltpu.make_async_copy(new_hbm, new_ref, small_sem.at[1])
    q_load.start()
    new_load.start()
    key_load.start()
    value_load = pltpu.make_async_copy(up_values_hbm.at[pl.ds(owned * 2, 2)], up_values, value_sem)

    def load(b):
        return pltpu.make_async_copy(cache_hbm.at[b], cache.at[b, pl.ds(0, width + rope)], load_sem.at[b])

    swap = (iota((rope, rope), 0) == lax.rem(iota((rope, rope), 1) + rope // 2, rope)).astype(jnp.bfloat16)
    grid_row = iota((steps * requests, rope), 0)
    grid = lax.div(grid_row, requests)
    for b in range(requests):
        grid = grid + jnp.where(lax.rem(grid_row, requests) == b, positions[b], 0)
    cosine, sine = cos_sin(grid.astype(jnp.float32) * frequency_ref[...])
    sine = jnp.where(iota((steps * requests, rope), 1) < rope // 2, -sine, sine)
    q_load.wait()
    flat = q_ref[...].reshape(steps * requests * heads, query_width)
    q_rope = flat[:, nope:]
    swapped = jnp.dot(q_rope, swap, preferred_element_type=jnp.float32)
    three = (steps * requests, heads, rope)
    rotated = (
        q_rope.astype(jnp.float32).reshape(three) * cosine[:, None, :] + swapped.reshape(three) * sine[:, None, :]
    )
    rotated = rotated.astype(jnp.bfloat16).reshape(steps * requests * heads, rope)
    rotated = jnp.concatenate([rotated, jnp.zeros_like(rotated)], axis=1)
    count = steps * requests * heads
    row = iota((count, count), 0)
    wanted = (row & (steps - 1)) * (requests * heads) + lax.div(row, rows) * heads + lax.div(lax.rem(row, rows), steps)
    order = (iota((count, count), 1) == wanted).astype(jnp.bfloat16)
    q_nope = jnp.dot(order, flat[:, :nope], preferred_element_type=jnp.float32).astype(jnp.bfloat16)
    rotated = jnp.dot(order, rotated, preferred_element_type=jnp.float32).astype(jnp.bfloat16)

    new_load.wait()
    new_flat = new_ref[...].astype(jnp.float32).reshape(steps * requests, width + rope).astype(jnp.bfloat16)
    new_rope = new_flat[:, width:]
    new_swapped = jnp.dot(new_rope, swap, preferred_element_type=jnp.float32)
    new_rotated = new_rope.astype(jnp.float32) * cosine + new_swapped * sine
    new_keys[...] = jnp.zeros_like(new_keys)
    new_keys[: steps * requests, :width] = new_flat[:, :width]
    new_keys[: steps * requests, width : width + rope] = new_rotated.astype(jnp.bfloat16)

    own_head = lax.div(lax.rem(iota((count, nope), 0), rows), steps)
    spread = jnp.concatenate(
        [jnp.where(own_head == h, q_nope.astype(jnp.float32), 0.0).astype(jnp.bfloat16) for h in range(heads)], axis=1
    )
    key_load.wait()
    for b in range(requests):
        load(b).start()
    value_load.start()
    latent = jnp.dot(spread, up_keys[...].reshape(heads * nope, width), preferred_element_type=jnp.float32)
    latent = latent.astype(jnp.bfloat16)
    for b in range(requests):
        queries[b, head, :, :width] = latent[b * rows : (b + 1) * rows]
        queries[b, head, :, width : width + tile] = rotated[b * rows : (b + 1) * rows]
        cache[b, width + rope :, :] = jnp.zeros((tile - rope, rows_cached), jnp.bfloat16)

    def remote(source, target, send, recv, device):
        return pltpu.make_async_remote_copy(
            src_ref=source, dst_ref=target, send_sem=send, recv_sem=recv, device_id=device, device_id_type=MESH
        )

    def q_near(b):
        block = queries.at[b, head]
        return remote(block, block, q1_send.at[b], q1_recv.at[b], at_head(near))

    def part_of(b, h, part):
        return queries.at[b, h, pl.ds(pl.multiple_of(part * (rows // 2), rows // 2), rows // 2)]

    def q_across(b):
        block = queries.at[b, head] if b == 0 else part_of(b, head, side)
        return remote(block, block, qy_send.at[b], qy_recv.at[b], at_head(across))

    def q_side(b):
        block = part_of(b, across, side)
        return remote(block, block, qx_send.at[b], qx_recv.at[b], (seq + 1 - 2 * side, head))

    def q_forward(b, last=False):
        if b == 0:
            block = queries.at[b, across]
        else:
            block = part_of(b, across, 1 - side if last else side)
        at = 2 * b + last
        return remote(block, block, qf_send.at[at], qf_recv.at[at], at_head(near))

    def a_copy(b, j):
        return remote(
            partial.at[b, 1 - low + 2 * j], a_in.at[b, j], a_send.at[b, j], a_recv.at[b, j], at_head(near)
        )

    def b_copy(b):
        return remote(b_out.at[b], b_in.at[b], b_send.at[b], b_recv.at[b], at_head(across))

    def c_copy(p, target, source):
        return remote(
            c_out.at[p, target], c_in.at[p, source], c_send.at[p, target], c_recv.at[p, source], (target, head)
        )

    def g_copy(d):
        target = lax.rem(seq + d, seq_size)
        return remote(
            gathered.at[owned], gathered.at[owned], g_send.at[target], g_recv.at[owned], (target, head)
        )

    pl.semaphore_wait(barrier, 2 + seq_size - 1)
    for b in range(requests):
        q_across(b).start()
    for b in range(requests):
        q_near(b).start()

    term, to_total = iota((tile, 2 * tile), 0), iota((tile, 2 * tile), 1) >= tile
    terms = (~to_total & (term < 3)) | (to_total & (term >= 3) & (term < 5))
    ones_at = jnp.where(terms, 1.0, 0.0).astype(jnp.bfloat16)

    factor = log2_e * float(query_width) ** (-0.5)
    nt = (((1,), (1,)), ((), ()))
    spans = [slice(c * chunk, (c + 1) * chunk) for c in range(rows_cached // chunk)]

    def tiles(x, op, start):
        for i in range(x.shape[1] // tile):
            start = op(start, x[:, i * tile : (i + 1) * tile])
        return start

    def forward(b):
        q_across(b).wait_recv()
        if b > 0:
            q_side(b).start()
        q_forward(b).start()

    def forward_rest(b):
        q_side(b).wait_recv()
        q_forward(b, True).start()

    def ready(b):
        q_near(b).wait_recv()
        q_forward(b).wait_recv()
        if b > 0:
            q_forward(b, True).wait_recv()
        load(b).wait()

    def score(b, span, peaks):
        q = queries[b].reshape(all_rows, width + tile)
        s = jnp.dot(q, cache[b, :, span], preferred_element_type=jnp.float32)
        number = slot * rows_cached + span.start + iota((1, chunk), 1)
        x = s * factor + jnp.where(number < lengths[b], 0.0, masked_score)
        scores[b % 2, :, span] = x
        return tiles(x, jnp.maximum, peaks)

    def score_new(b, peaks):
        q = queries[b].reshape(all_rows, width + tile)
        s = lax.dot_general(q, new_keys[...], nt, preferred_element_type=jnp.float32)
        column = iota((all_rows, tile), 1)
        step = iota((all_rows, tile), 0) & (steps - 1)
        fresh = (
            (lax.rem(column, requests) == b)
            & (lax.div(column, requests) <= step)
            & (column < steps * requests)
            & (slot == 0)
        )
        x = s * factor + jnp.where(fresh, 0.0, masked_score)
        peak = jnp.max(jnp.maximum(peaks, x), axis=1, keepdims=True)
        return x, jnp.broadcast_to(peak, (all_rows, tile))

    lowest = jnp.full((all_rows, tile), lowest_peak, jnp.float32)

    def attend(b, x_new, peak):
        more = b + 1 < requests
        peaks = lowest
        fresh = jnp.exp2(x_new - peak)
        totals = fresh
        for span in spans:
            if more:
                peaks = score(b + 1, span, peaks)
            w = jnp.exp2(scores[b % 2, :, span] - jnp.concatenate([peak] * (chunk // tile), axis=1))
            totals = tiles(w, jnp.add, totals)
            weights[:, span] = w.astype(jnp.bfloat16)
        if b + 2 < requests:
            forward_rest(b + 2)
        if b + 3 < requests:
            forward(b + 3)
        if b >= 1:
            merge_near(b - 1)
        if b >= 2:
            merge_across(b - 2)
        following = score_new(b + 1, peaks) if more else None
        mixed = jnp.dot(fresh.astype(jnp.bfloat16), new_keys[:, :width], preferred_element_type=jnp.float32)
        mixed += lax.dot_general(weights[...], cache[b, :width, :], nt, preferred_element_type=jnp.float32)
        values, stats = pack(mixed, peak, jnp.broadcast_to(jnp.sum(totals, axis=1, keepdims=True), peak.shape))
        partial[b, :, :, :width] = values.reshape(4, rows, width)
        partial[b, :, :, width:] = stats.reshape(4, rows, tile)
        for j in range(2):
            a_copy(b, j).start()
        if b >= 3:
            finish(b - 3)
        return following

    def merge_near(b):
        for j in range(2):
            a_copy(b, j).wait_recv()
        other = 1 - high
        merged = merge(
            unpack(partial[b, low + 2 * other], width, ones_at),
            unpack(a_in[b, other], width, ones_at),
        )
        values, stats = pack(*merged)
        b_out[b, :, :width] = values
        b_out[b, :, width:] = stats
        b_copy(b).start()
        values, peak, total = merge(
            unpack(partial[b, head], width, ones_at),
            unpack(a_in[b, high], width, ones_at),
        )
        kept[b, :, :width] = values
        kept[b, :, width : width + tile] = peak
        kept[b, :, width + tile :] = total

    def merge_across(b):
        b_copy(b).wait_recv()
        mine = (kept[b, :, :width], kept[b, :, width : width + tile], kept[b, :, width + tile :])
        values, stats = pack(*merge(mine, unpack(b_in[b], width, ones_at)))
        values = values.astype(jnp.float32).reshape(owners, piece, width)
        stats = stats.astype(jnp.float32).reshape(owners, piece, tile)
        c_out[b, :, :, :half] = jnp.concatenate([values[..., :half], values[..., half:]], axis=1).astype(jnp.bfloat16)
        c_out[b, :, :, half:] = jnp.concatenate([stats, stats], axis=1).astype(jnp.bfloat16)
        for d in range(0 if seq_size > owners else 1, owners):
            target = lax.rem(seq + d, owners)
            if d == 0:
                @pl.when(seq >= owners)
                def _():
                    c_copy(b, target, seq).start()
            else:
                c_copy(b, target, seq).start()

    def when_owner(fn):
        if seq_size > owners:
            pl.when(seq < owners)(fn)
        else:
            fn()

    def finish(b):
        def combine():
            c_in[b, owned] = c_out[b, owned]
            for d in range(1, seq_size):
                c_copy(b, owned, lax.rem(seq + d, seq_size)).wait_recv()
            values, peaks, totals = unpack(c_in[b], half, ones_at)
            peak = jnp.max(peaks, axis=0, keepdims=True)
            scale = jnp.exp2(peaks - peak)
            mixed = by_tile(jnp.sum(by_tile(values, scale), axis=0), 1.0 / jnp.sum(totals * scale, axis=0))
            mixed_latent[b, :, :half] = mixed[:piece]
            mixed_latent[b, :, half:] = mixed[piece:]

        when_owner(combine)

    def project():
        mixed = mixed_latent[...].reshape(requests * piece, width)
        second = lax.rem(iota(mixed.shape, 0), piece) >= steps
        wide = jnp.concatenate([jnp.where(second, 0.0, mixed), jnp.where(second, mixed, 0.0)], axis=1)
        w0 = wide.astype(jnp.bfloat16)
        rest = wide - w0.astype(jnp.float32)
        w1 = rest.astype(jnp.bfloat16)
        w2 = (rest - w1.astype(jnp.float32)).astype(jnp.bfloat16)
        matrix = up_values[...].reshape(2 * width, up_values.shape[2])
        result = sum(jnp.dot(w, matrix, preferred_element_type=jnp.float32) for w in (w2, w1, w0))
        gathered[owned] = result.astype(jnp.bfloat16)

    forward(0)
    forward(1)
    ready(0)
    peaks = lowest
    for span in spans:
        peaks = score(0, span, peaks)
    following = score_new(0, peaks)
    forward_rest(1)
    forward(2)
    for b in range(requests):
        if b + 1 < requests:
            ready(b + 1)
        following = attend(b, *following)
    merge_near(requests - 1)
    merge_across(requests - 2)
    finish(requests - 3)
    value_load.wait()
    merge_across(requests - 1)
    finish(requests - 2)
    finish(requests - 1)

    def last():
        project()
        for d in range(1, seq_size):
            g_copy(d).start()

    when_owner(last)

    def from_owner(j):
        block = gathered.at[j]
        return remote(block, block, g_send.at[j], g_recv.at[j], (seq, near))

    for d in range(0 if seq_size > owners else 1, owners):
        source = lax.rem(seq + d, owners)
        if d == 0:
            @pl.when(seq >= owners)
            def _():
                from_owner(source).wait_recv()
        else:
            from_owner(source).wait_recv()

    per = rows * requests // owners
    row = iota((count, count), 0)
    s_of = lax.div(row, requests * heads)
    b_of = lax.rem(lax.div(row, heads), requests)
    h_of = lax.rem(row, heads)
    source = lax.div(h_of, 2) * per + b_of * piece + (h_of & 1) * steps + s_of
    back = (iota((count, count), 1) == source).astype(jnp.bfloat16)
    result = jnp.dot(back, gathered[...].reshape(count, -1), preferred_element_type=jnp.float32)
    out_ref[...] = result.reshape(out_ref.shape)

    for b in range(requests):
        q_near(b).wait_send()
        q_across(b).wait_send()
        q_forward(b).wait_send()
        if b > 0:
            q_side(b).wait_send()
            q_forward(b, True).wait_send()
        for j in range(2):
            a_copy(b, j).wait_send()
        b_copy(b).wait_send()
    for p in range(requests):
        for d in range(0 if seq_size > owners else 1, owners):
            target = lax.rem(seq + d, owners)
            if d == 0:
                @pl.when(seq >= owners)
                def _():
                    c_copy(p, target, seq).wait_send()
            else:
                c_copy(p, target, seq).wait_send()

    def sent():
        for d in range(1, seq_size):
            g_copy(d).wait_send()

    when_owner(sent)


def on_device(seq_size, query_heads, up_keys, up_values, latent_cache, new_latent, context_lengths, positions):
    steps, requests, heads, query_width = query_heads.shape
    nope, width = up_keys.shape[1:]
    value_width = up_values.shape[2]
    key_width = latent_cache.shape[2]
    cached = latent_cache.shape[1]
    rows = steps * heads
    bf16, f32 = jnp.bfloat16, jnp.float32
    packed = width + tile
    dma = pltpu.SemaphoreType.DMA
    smem = pl.BlockSpec(memory_space=pltpu.SMEM)
    vmem = pl.BlockSpec(memory_space=pltpu.VMEM)
    anywhere = pl.BlockSpec(memory_space=pl.ANY)
    attended = pl.pallas_call(
        functools.partial(kernel, seq_size),
        out_shape=pltpu.VMEM((steps, requests, heads, value_width), f32),
        in_specs=[smem, smem, anywhere, anywhere, vmem, anywhere, anywhere, anywhere],
        out_specs=vmem,
        scratch_shapes=[
            pltpu.VMEM(query_heads.shape, bf16),
            pltpu.VMEM(new_latent.shape, bf16),
            pltpu.VMEM((heads, nope, width), bf16),
            pltpu.VMEM((2, width, value_width), bf16),
            pltpu.VMEM((requests, packed, cached), bf16),
            pltpu.VMEM((requests, 4, rows, packed), bf16),
            pltpu.VMEM((tile, packed), bf16),
            pltpu.VMEM((2, 4 * rows, cached), f32),
            pltpu.VMEM((4 * rows, cached), bf16),
            pltpu.VMEM((requests, 4, rows, packed), bf16),
            pltpu.VMEM((requests, 2, rows, packed), bf16),
            pltpu.VMEM((requests, rows, packed), bf16),
            pltpu.VMEM((requests, rows, packed + tile), f32),
            pltpu.VMEM((requests, rows, packed), bf16),
            pltpu.VMEM((requests, owners, 2 * rows // owners, width // 2 + tile), bf16),
            pltpu.VMEM((requests, seq_size, 2 * rows // owners, width // 2 + tile), bf16),
            pltpu.VMEM((requests, rows // owners, width), f32),
            pltpu.VMEM((owners, requests * rows // owners, value_width), bf16),
            dma((2,)),
            dma((requests,)),
            dma,
            dma,
        ]
        + [dma((requests,))] * 4
        + [dma((2 * requests,))] * 2
        + [dma((requests,))] * 2
        + [dma((requests, 2))] * 2
        + [dma((requests,))] * 2
        + [dma((requests, owners)), dma((requests, seq_size)), dma((seq_size,)), dma((owners,))],
        compiler_params=pltpu.CompilerParams(
            collective_id=0, has_side_effects=True, vmem_limit_bytes=56 * 1024 * 1024
        ),
        cost_estimate=pl.CostEstimate(
            flops=2 * requests * 4 * rows * cached * (key_width + width),
            bytes_accessed=2 * requests * cached * key_width,
            transcendentals=requests * 4 * rows * cached,
        ),
    )(
        context_lengths,
        positions,
        query_heads,
        new_latent,
        jnp.asarray(frequencies(query_width - nope)),
        up_keys,
        up_values,
        jnp.swapaxes(latent_cache, 1, 2),
    )
    return attended.astype(bf16)


def solution(mesh):
    in_specs = (
        P(None, None, "head", None),
        P("head", None, None),
        P("head", None, None),
        P(None, ("seq", "head"), None),
        P(),
        P(),
        P(),
    )
    out_specs = P(None, None, "head", None)
    return jax.shard_map(
        functools.partial(on_device, mesh.shape["seq"]),
        mesh=mesh,
        in_specs=in_specs,
        out_specs=out_specs,
        check_vma=False,
    )
```
